32 devices in a mesh: groups: 2 (over x), rows: 16 (over z, y, core).
Axes of the slice: x: 2, y: 2, z: 4, core: 2. Of those that a mesh axis runs over, the one named last changes fastest.
Arguments:
- features: bfloat16 [131072, 1024], P(('groups', 'rows')), parts along dimension 0, may hold values from -6 to 6
- coef: bfloat16 [1024], replicated, may hold values from -0.1875 to 0.1875
- labels: int32 [131072], P(('groups', 'rows')), parts along dimension 0, may hold values 0 or 1
- passage_id: int32 [131072, 1], P(('groups', 'rows')), parts along dimension 0, may hold values from 0 to 127; in each aligned block of 4096 rows (0 to 4095, 4096 to 8191, ...) at most 64 rows name the same one
- slot_of: int32 [256], P('groups'), parts along dimension 0, may hold values from 0 to 127, each once
Outputs:
- hessian: float32 [2048, 1024], P(('groups', 'rows')), parts along dimension 0
- meat: float32 [2048, 1024], P(('groups', 'rows')), parts along dimension 0
- grad_sums: float32 [256, 1024], P(('groups', 'rows')), parts along dimension 0
The draws below stay inside these ranges and needn't reach their ends.
There are 2 independent parts, one for each index of `groups`. The reference program is written for one: setup_inputs(seed, part) draws one part's arguments, and reference() takes and returns one part's arrays. A program takes and returns all parts, laid end to end along the dimension named above; an argument that names none is the same for every part. Nothing has to cross between parts.
Inputs may be any that keep to these rules, and one draw needn't show every extreme that they name: `passage_id`: on one device's rows each passage is named at most 64 times; every passage is named somewhere. `slot_of`: each slot once.
All inputs are finite; a program needn't handle non-finite values. No bound on the sum of `labels` on one device may be relied on, other than what follows from the above.
Results may differ from the reference program's by a relative error of at most 0.0028.
Values may be sent and summed in bfloat16 or wider, within the bound.
No kernel may reach another device: no remote copies, remote signals or barrier semaphores. Data moves between devices by JAX's collectives and lax.ppermute only.
A program may use at most 128 MiB of HBM per device.

```python
import math
import jax
import jax.numpy as jnp
import numpy as np
from jax import lax

F = 1024
ROWS_DEV = 4096
ROWS = 65536
CLUSTERS = 128
MOST = 64
N_ROWS = 16


def set_ends(drawn, key, smallest, top_value):
    spot = [jax.random.randint(jax.random.fold_in(key, axis), (), 0, length) for axis, length in enumerate(drawn.shape)]
    widest = drawn.shape.index(max(drawn.shape))
    beside = spot[:widest] + [(spot[widest] + 1) % drawn.shape[widest]] + spot[widest + 1:]
    return drawn.at[tuple(spot)].set(smallest).at[tuple(beside)].set(top_value)


def raised(entries, own_key, source, target, parts, factor):
    def block_of(axis_at):
        return (jnp.arange(entries.shape[axis_at]) // (entries.shape[axis_at] // parts)).reshape((-1,) + (1,) * (entries.ndim - 1 - axis_at))

    near = jax.random.permutation(own_key, parts)[block_of(target)]
    far = (block_of(target) + parts // 2) % parts
    return jnp.where((block_of(source) == near) | (block_of(source) == far), factor * entries, entries)


def steps_of(stream_key, dims, shards, low, high):
    level = 1.0
    for dim, blocks in shards:
        steps = jax.random.uniform(jax.random.fold_in(jax.random.fold_in(stream_key, 6), dim), (blocks,), jnp.float32, low / len(shards), high / len(shards))
        level = level * jnp.repeat(jnp.exp(steps), dims[dim] // blocks).reshape((-1,) + (1,) * (len(dims) - 1 - dim))
    return level


def routed_block(own_key, own, number, rows, amount, top, limit, slope):
    order = jax.random.permutation(own_key, amount)
    crowded, usual = portions_of(amount, rows * top, limit, slope, True), portions_of(amount, rows * top, limit, slope, False)
    places = jnp.arange(amount)

    def named(sizes, rotation):
        used = int((sizes > 0).sum())
        fixed = max(1, used // 4)
        shifted = fixed + (places - fixed + rotation * (used - fixed)) % max(1, amount - fixed)
        return jnp.zeros((amount,), jnp.int32).at[order[jnp.where(places < fixed, places, shifted)]].set(jnp.asarray(sizes, jnp.int32))

    sizes = jnp.where(number % 4 == 0, named(crowded, number // 4), named(usual, number - number // 4 - 1))
    mixed = jax.random.permutation(jax.random.fold_in(own, 3), amount)
    donor, sink = mixed[0:amount // 2 * 2:2], mixed[1:amount // 2 * 2:2]
    slack = jnp.minimum(sizes[donor] - 1, limit - sizes[sink]) // 2
    slack = jnp.where((donor == order[0]) | (sink == order[0]) | (sizes[sink] == 0), 0, jnp.maximum(slack, 0))
    shifted = jax.random.randint(jax.random.fold_in(own, 4), (amount // 2,), 0, 1 << 20) % (slack + 1)
    sizes = sizes.at[donor].add(-shifted).at[sink].add(shifted)
    items = jnp.searchsorted(jnp.cumsum(sizes), jnp.arange(rows * top), side="right").astype(jnp.int32)
    grid = items.reshape(top, rows).T
    grid = grid[jax.random.permutation(jax.random.fold_in(own, 1), rows)]
    rotation = jax.random.randint(jax.random.fold_in(own, 2), (rows, 1), 0, top)
    return jnp.take_along_axis(grid, (jnp.arange(top)[None, :] + rotation) % top, axis=1)


def portions_of(number_of, total, most, lean, full):
    portions = [(1 << 20) // math.isqrt(rank ** lean) + 1 for rank in range(1, number_of + 1)]
    largest = most if full else min(most, max(-(-total // number_of), total * portions[0] // sum(portions)))
    least = 1 if total - largest >= number_of - 1 else 0
    counts, spare = [largest] + [least] * (number_of - 1), total - largest - least * (number_of - 1)
    while spare > 0:
        movable = [i for i in range(1, number_of) if counts[i] < largest] or [i for i in range(1, number_of) if counts[i] < most]
        pool, left = sum([portions[i] for i in movable]), spare
        for i in movable:
            addition = min(most - counts[i], max(1, left * portions[i] // pool), spare)
            counts[i] = counts[i] + addition
            spare = spare - addition
    return np.array(counts)


def noise(key, extent, width, most, shards=(), held_as=jnp.bfloat16):
    factor_of = steps_of(key, extent, shards, -0.22, 0.18) if shards else 1.0
    array = jax.random.normal(key, extent, jnp.float32) * width * factor_of
    return jnp.minimum(jnp.maximum(array, -most), most).astype(held_as)


def gaussian_with(own_key, shape, width, reach, shards, heavy, held_as=jnp.bfloat16):
    values = width * jax.random.normal(own_key, shape, jnp.float32)
    if shards:
        values = values * steps_of(own_key, shape, shards, -0.22, 0.18)
    return jnp.clip(raised(values, jax.random.fold_in(own_key, 3), *heavy), -reach, reach).astype(held_as)


def setup_inputs(seed: int = 0, part: int = 0) -> dict:
    streams_of = jax.random.split(jax.random.key(seed), 6)
    own_keys = jax.random.split(jax.random.fold_in(streams_of[5], part), 6)
    features = gaussian_with(own_keys[0], (ROWS, F), 1.0, 6.0, ((0, 16),), (0, 1, 16, 2.0))
    coef = noise(streams_of[1], (F,), F ** -0.5, 0.1875)
    labels = set_ends((jax.random.randint(own_keys[2], (ROWS,), 0, 2) < 1).astype(jnp.int32), jax.random.fold_in(own_keys[2], 1), 0, 1)
    passage_id_keys = jax.random.split(jax.random.fold_in(own_keys[3], 1), ROWS // ROWS_DEV)
    passage_id_turns = jax.random.permutation(jax.random.fold_in(own_keys[3], 3), ROWS // ROWS_DEV)
    passage_id = jax.vmap(lambda own, number: routed_block(jax.random.fold_in(own_keys[3], 2), own, number, ROWS_DEV, CLUSTERS, 1, MOST, 2))(passage_id_keys, passage_id_turns).reshape((ROWS, 1))
    slot_of = jax.random.permutation(own_keys[4], CLUSTERS).astype(jnp.int32)
    return dict(features=features, coef=coef, labels=labels, passage_id=passage_id, slot_of=slot_of)


def reference(features, coef, labels, passage_id, slot_of):
    feat_dim = features.shape[1]
    slot_row = jnp.take(slot_of, passage_id[:, 0]).astype(jnp.int32)
    feat_blocks = features.reshape(N_ROWS, ROWS_DEV, feat_dim)
    label_blocks = labels.reshape(N_ROWS, ROWS_DEV)
    slot_blocks = slot_row.reshape(N_ROWS, ROWS_DEV)

    def step_block(carry, inputs):
        hess_acc, sums_acc = carry
        feat_block, label_block, slot_block = inputs
        logits = jnp.dot(feat_block, coef, preferred_element_type=jnp.float32)
        probability = jax.nn.sigmoid(logits)
        weighted = (feat_block.astype(jnp.float32) * (probability * (1.0 - probability))[:, None]).astype(jnp.bfloat16)
        scored = (feat_block.astype(jnp.float32) * (label_block.astype(jnp.float32) - probability)[:, None]).astype(jnp.bfloat16)
        hess_acc = hess_acc + jnp.dot(feat_block.astype(jnp.float32).T, weighted.astype(jnp.float32), precision=lax.Precision.HIGHEST)
        sums_acc = sums_acc + jax.ops.segment_sum(scored.astype(jnp.float32), slot_block, CLUSTERS)
        return (hess_acc, sums_acc), None

    start_carry = (jnp.zeros((feat_dim, feat_dim), jnp.float32), jnp.zeros((CLUSTERS, feat_dim), jnp.float32))
    (hessian, grad_sums), _ = lax.scan(step_block, start_carry, (feat_blocks, label_blocks, slot_blocks))
    meat = jnp.dot(grad_sums.T, grad_sums, precision=lax.Precision.HIGHEST)
    return (hessian, meat, grad_sums)
```

```python
import functools

import jax
import jax.numpy as jnp
from jax import lax
from jax.experimental import pallas as pl
from jax.experimental.pallas import tpu as pltpu
from jax.sharding import PartitionSpec as P

BF16 = jnp.bfloat16
F32 = jnp.float32
LANES = 128
VMEM_LIMIT = 48 * 1024 * 1024


def score_kernel(
    per_owner, place, x_ref, coef_ref, label_ref, pid_ref, slot_ref, w_ref, send_ref, keep_ref, names
):
    step = pl.program_id(0)
    clusters = slot_ref.shape[1]
    half = clusters // 2

    @pl.when(step == 0)
    def _():
        core = place[0]
        row = lax.broadcasted_iota(jnp.int32, (clusters, clusters), 0)
        mine = row >= half
        inner = jnp.where(mine, row - half, row)
        slot = (2 * (inner // per_owner) + jnp.where(mine, core, 1 - core)) * per_owner + inner % per_owner
        passage = lax.broadcasted_iota(jnp.int32, (clusters, clusters), 1)
        found = jnp.where(slot_ref[...] == slot, passage, 0)
        names[...] = jnp.broadcast_to(jnp.sum(found, axis=1, keepdims=True), names.shape)
        send_ref[...] = jnp.zeros_like(send_ref)
        keep_ref[...] = jnp.zeros_like(keep_ref)

    x = x_ref[...]
    rows = x.shape[0]
    coef = jnp.broadcast_to(coef_ref[...], (16, x.shape[1]))
    logits = lax.dot_general(coef, x, (((1,), (1,)), ((), ())), preferred_element_type=F32)[0:1]
    prob = 1.0 / (1.0 + jnp.exp(-logits))
    w_ref[...] = prob * (1.0 - prob)
    score = label_ref[...].astype(F32) - prob
    score = jnp.broadcast_to(score, (LANES, rows)).T
    wide = x.shape[1] // LANES
    scored = (x.astype(F32) * jnp.concatenate([score] * wide, axis=1)).astype(BF16)
    member = jnp.where(pid_ref[...] == names[:, 0:1], 1.0, 0.0).astype(BF16)
    sums = jnp.dot(member, scored, preferred_element_type=F32)
    send_ref[...] += sums[:half]
    keep_ref[...] += sums[half:]


def hessian_kernel(blk, place, x_ref, w_ref, send_ref, keep_ref, acc):
    step = pl.program_id(0)
    feat = x_ref.shape[1]
    parity, core = place[0], place[1]
    weight = w_ref[...]
    left = []
    for block in range(feat // (2 * LANES)):
        start = pl.multiple_of((2 * block + parity) * LANES, LANES)
        turned = x_ref[:, pl.ds(start, LANES)].astype(F32).T
        left.append((turned * weight).astype(BF16))
    term = jnp.dot(jnp.concatenate(left, axis=0), x_ref[...], preferred_element_type=F32)

    @pl.when(step == 0)
    def _():
        acc[...] = term

    @pl.when(step > 0)
    def _():
        acc[...] += term

    @pl.when(step == pl.num_programs(0) - 1)
    def _():
        for pair in range(acc.shape[0] // (2 * blk)):
            base = pair * 2 * blk
            out = pl.ds(pair * blk, blk)
            keep_ref[out, :] = acc[pl.ds(pl.multiple_of(base + core * blk, 8), blk), :]
            send_ref[out, :] = acc[pl.ds(pl.multiple_of(base + (1 - core) * blk, 8), blk), :].astype(BF16)


def scores(place, x, coef, labels, pid, slot_of, per_owner, tile=512):
    rows, feat = x.shape
    clusters = slot_of.shape[0]
    half = clusters // 2
    whole = lambda shape: pl.BlockSpec(shape, lambda i: (0, 0))
    return pl.pallas_call(
        functools.partial(score_kernel, per_owner),
        grid=(rows // tile,),
        in_specs=[
            pl.BlockSpec(memory_space=pltpu.SMEM),
            pl.BlockSpec((tile, feat), lambda i: (i, 0)),
            whole((1, feat)),
            pl.BlockSpec((1, tile), lambda i: (0, i)),
            pl.BlockSpec((1, tile), lambda i: (0, i)),
            whole((1, clusters)),
        ],
        out_specs=[pl.BlockSpec((1, tile), lambda i: (0, i)), whole((half, feat)), whole((half, feat))],
        out_shape=[
            jax.ShapeDtypeStruct((1, rows), F32),
            jax.ShapeDtypeStruct((half, feat), F32),
            jax.ShapeDtypeStruct((half, feat), F32),
        ],
        scratch_shapes=[pltpu.VMEM((clusters, LANES), jnp.int32)],
        compiler_params=pltpu.CompilerParams(vmem_limit_bytes=VMEM_LIMIT),
        name="scores",
    )(place, x, coef.reshape(1, feat), labels.reshape(1, rows), pid.reshape(1, rows), slot_of.reshape(1, clusters))


def hessian_half(place, x, w, blk, tile=1024):
    rows, feat = x.shape
    half, quarter = feat // 2, feat // 4
    whole = lambda shape: pl.BlockSpec(shape, lambda i: (0, 0))
    return pl.pallas_call(
        functools.partial(hessian_kernel, blk),
        grid=(rows // tile,),
        in_specs=[
            pl.BlockSpec(memory_space=pltpu.SMEM),
            pl.BlockSpec((tile, feat), lambda i: (i, 0)),
            pl.BlockSpec((1, tile), lambda i: (0, i)),
        ],
        out_specs=[whole((quarter, feat)), whole((quarter, feat))],
        out_shape=[
            jax.ShapeDtypeStruct((quarter, feat), BF16),
            jax.ShapeDtypeStruct((quarter, feat), F32),
        ],
        scratch_shapes=[pltpu.VMEM((half, feat), F32)],
        compiler_params=pltpu.CompilerParams(vmem_limit_bytes=VMEM_LIMIT),
        name="hessian_half",
    )(place, x, w)


def local(features, coef, labels, passage_id, slot_of):
    feat = features.shape[1]
    devices = lax.axis_size("rows")
    clusters = slot_of.shape[0]
    per_owner = clusters // devices
    blk = feat // devices
    me = lax.axis_index("rows")
    turn = LANES // blk
    core, parity = me % 2, (me // turn) % 2

    def swap(array, mask):
        return lax.ppermute(array, "rows", [(i, i ^ mask) for i in range(devices)])

    def rest(number):
        return (number // (2 * turn)) * (turn // 2) + (number % turn) // 2

    core_ref = core.astype(jnp.int32).reshape(1)
    w, sums_send, sums_keep = scores(core_ref, features, coef, labels, passage_id, slot_of, per_owner)
    sums = sums_keep + swap(sums_send, 1)
    masks = [m for m in range(1, devices) if not m & 1 and not m & turn]
    members = [
        [base ^ m for m in [0] + masks]
        for base in range(devices)
        if not rest(base)
    ]
    gathered = lax.all_gather(sums.astype(BF16), "rows", axis=0, axis_index_groups=members)

    far_send, far_keep = hessian_half(jnp.stack([1 - parity, core]), features, w, blk)
    far = (far_keep + swap(far_send, 1).astype(F32)).astype(BF16)
    arrived = swap(far, turn)
    near_send, near_keep = hessian_half(jnp.stack([parity, core]), features, w, blk)
    near = near_keep + swap(near_send, 1).astype(F32) + arrived.astype(F32)
    mine = rest(me)
    block = lambda n: lax.dynamic_slice_in_dim(near, n * blk, blk, 0)
    hessian = block(mine)
    parts = [swap(block(mine ^ rest(m)).astype(BF16), m) for m in masks]

    sums = jnp.sum(gathered.astype(F32), axis=0)
    sums = sums + swap(sums, turn)
    other = swap(sums, 1)
    chip = me // 2
    grad_local = lax.dynamic_slice_in_dim(sums, chip * per_owner, per_owner, 0)
    stack = jnp.concatenate([sums, other], axis=0)
    columns = lax.dynamic_slice_in_dim(stack, me * blk, blk, 1)
    meat = lax.dot_general(
        columns,
        stack,
        (((0,), (0,)), ((), ())),
        precision=lax.Precision.HIGHEST,
        preferred_element_type=F32,
    )
    for part in parts:
        hessian = hessian + part.astype(F32)
    return (hessian, meat, grad_local)


def solution(mesh):
    in_specs = (
        P(("groups", "rows"), None),
        P(),
        P(("groups", "rows")),
        P(("groups", "rows"), None),
        P("groups"),
    )
    out_specs = (
        P(("groups", "rows"), None),
        P(("groups", "rows"), None),
        P(("groups", "rows"), None),
    )
    return jax.shard_map(local, mesh=mesh, in_specs=in_specs, out_specs=out_specs, check_vma=False)
```

```python
import functools

import jax
import jax.numpy as jnp
from jax import lax
from jax.experimental import pallas as pl
from jax.experimental.pallas import tpu as pltpu
from jax.sharding import PartitionSpec as P

BF16 = jnp.bfloat16
F32 = jnp.float32
LANES = 128
VMEM_LIMIT = 40 * 1024 * 1024


def blocks_of(x_ref, start, rows, parity, weight):
    left = []
    for block in range(x_ref.shape[1] // (2 * LANES)):
        lane = pl.multiple_of((2 * block + parity) * LANES, LANES)
        turned = x_ref[start : start + rows, pl.ds(lane, LANES)].T
        left.append((turned.astype(F32) * weight).astype(BF16))
    return jnp.concatenate(left, axis=0)


def split_by_core(blk, core, acc, send_ref, keep_ref):
    for pair in range(acc.shape[0] // (2 * blk)):
        base = pair * 2 * blk
        out = pl.ds(pair * blk, blk)
        keep_ref[out, :] = acc[pl.ds(pl.multiple_of(base + core * blk, 8), blk), :]
        send_ref[out, :] = acc[pl.ds(pl.multiple_of(base + (1 - core) * blk, 8), blk), :].astype(BF16)


def first_kernel(
    per_owner, blk, chunks, place, x_hbm, coef_hbm, label_hbm, pid_hbm, slot_hbm,
    x_ref, w_ref, sums_send, sums_keep, send_ref, keep_ref, cross_ref,
    acc, coef_ref, label_ref, pid_ref, slot_ref, x_sems, sems,
):
    core, parity = place[0], place[1]
    rows, feat = x_ref.shape
    clusters = slot_ref.shape[1]
    half = clusters // 2
    part = rows // chunks
    small = [
        pltpu.make_async_copy(source, target, sems.at[n])
        for n, (source, target) in enumerate(
            [(coef_hbm, coef_ref), (slot_hbm, slot_ref), (label_hbm, label_ref), (pid_hbm, pid_ref)]
        )
    ]
    large = [
        pltpu.make_async_copy(x_hbm.at[pl.ds(n * part, part)], x_ref.at[pl.ds(n * part, part)], x_sems.at[n])
        for n in range(chunks)
    ]
    for copy in small:
        copy.start()
    for copy in large:
        copy.start()
    for copy in small:
        copy.wait()
    row = lax.broadcasted_iota(jnp.int32, (clusters, clusters), 0)
    mine = row >= half
    inner = jnp.where(mine, row - half, row)
    slot = (2 * (inner // per_owner) + jnp.where(mine, core, 1 - core)) * per_owner + inner % per_owner
    passage = lax.broadcasted_iota(jnp.int32, (clusters, clusters), 1)
    names = jnp.sum(jnp.where(slot_ref[...] == slot, passage, 0), axis=1, keepdims=True)
    coef = jnp.broadcast_to(coef_ref[...].reshape(1, feat), (16, feat))
    for n in range(chunks):
        start = n * part
        here = slice(start, start + part)
        large[n].wait()
        x = x_ref[here, :]
        logits = lax.dot_general(coef, x, (((1,), (1,)), ((), ())), preferred_element_type=F32)[0:1]
        prob = 1.0 / (1.0 + jnp.exp(-logits))
        weight = prob * (1.0 - prob)
        w_ref[:, here] = weight
        score = label_ref[:, here].astype(F32) - prob
        score = jnp.broadcast_to(score, (LANES, part)).T
        scored = (x.astype(F32) * jnp.concatenate([score] * (feat // LANES), axis=1)).astype(BF16)
        member = jnp.where(pid_ref[:, here] == names, 1.0, 0.0).astype(BF16)
        sums = jnp.dot(member, scored, preferred_element_type=F32)
        term = jnp.dot(blocks_of(x_ref, start, part, 1 - parity, weight), x, preferred_element_type=F32)
        if n:
            sums_send[...] += sums[:half]
            sums_keep[...] += sums[half:]
            acc[...] += term
        else:
            sums_send[...] = sums[:half]
            sums_keep[...] = sums[half:]
            acc[...] = term
    split_by_core(blk, core, acc, send_ref, keep_ref)
    for block in range(feat // (2 * LANES)):
        lane = pl.multiple_of((2 * block + parity) * LANES, LANES)
        cross_ref[:, block * LANES : (block + 1) * LANES] = acc[:, pl.ds(lane, LANES)]


def second_kernel(blk, chunks, place, x_ref, w_ref, cross_ref, send_ref, keep_ref, acc):
    core, parity = place[0], place[1]
    rows, feat = x_ref.shape
    part = rows // chunks
    width = feat // (2 * LANES)
    total = None
    for n in range(chunks):
        start = n * part
        right = jnp.concatenate(
            [
                x_ref[start : start + part, pl.ds(pl.multiple_of((2 * b + parity) * LANES, LANES), LANES)]
                for b in range(width)
            ],
            axis=1,
        )
        left = blocks_of(x_ref, start, part, parity, w_ref[:, start : start + part])
        term = jnp.dot(left, right, preferred_element_type=F32)
        total = term if total is None else total + term
    turned = cross_ref[...].T
    for b in range(width):
        own = pl.multiple_of((2 * b + parity) * LANES, LANES)
        other = pl.multiple_of((2 * b + 1 - parity) * LANES, LANES)
        acc[:, pl.ds(own, LANES)] = total[:, b * LANES : (b + 1) * LANES]
        acc[:, pl.ds(other, LANES)] = turned[:, b * LANES : (b + 1) * LANES]
    split_by_core(blk, core, acc, send_ref, keep_ref)


VMEM_SPEC = pl.BlockSpec(memory_space=pltpu.VMEM)


def first(place, x, coef, labels, pid, slot_of, per_owner, blk, chunks=4):
    rows, feat = x.shape
    clusters = slot_of.shape[0]
    hbm = pl.BlockSpec(memory_space=pltpu.HBM)
    shape = jax.ShapeDtypeStruct
    return pl.pallas_call(
        functools.partial(first_kernel, per_owner, blk, chunks),
        in_specs=[pl.BlockSpec(memory_space=pltpu.SMEM)] + [hbm] * 5,
        out_specs=[VMEM_SPEC] * 7,
        out_shape=[
            shape((rows, feat), BF16),
            shape((1, rows), F32),
            shape((clusters // 2, feat), F32),
            shape((clusters // 2, feat), F32),
            shape((feat // 4, feat), BF16),
            shape((feat // 4, feat), F32),
            shape((feat // 2, feat // 2), F32),
        ],
        scratch_shapes=[
            pltpu.VMEM((feat // 2, feat), F32),
            pltpu.VMEM((feat,), BF16),
            pltpu.VMEM((1, rows), jnp.int32),
            pltpu.VMEM((1, rows), jnp.int32),
            pltpu.VMEM((1, clusters), jnp.int32),
            pltpu.SemaphoreType.DMA((chunks,)),
            pltpu.SemaphoreType.DMA((4,)),
        ],
        compiler_params=pltpu.CompilerParams(vmem_limit_bytes=VMEM_LIMIT),
        name="scores_and_far",
    )(place, x, coef, labels.reshape(1, rows), pid.reshape(1, rows), slot_of.reshape(1, clusters))


def second(place, x, w, cross, blk, chunks=4):
    rows, feat = x.shape
    return pl.pallas_call(
        functools.partial(second_kernel, blk, chunks),
        in_specs=[pl.BlockSpec(memory_space=pltpu.SMEM)] + [VMEM_SPEC] * 3,
        out_specs=[VMEM_SPEC] * 2,
        out_shape=[
            jax.ShapeDtypeStruct((feat // 4, feat), BF16),
            jax.ShapeDtypeStruct((feat // 4, feat), F32),
        ],
        scratch_shapes=[pltpu.VMEM((feat // 2, feat), F32)],
        compiler_params=pltpu.CompilerParams(vmem_limit_bytes=VMEM_LIMIT),
        name="near",
    )(place, x, w, cross)


def local(features, coef, labels, passage_id, slot_of):
    feat = features.shape[1]
    devices = lax.axis_size("rows")
    clusters = slot_of.shape[0]
    per_owner = clusters // devices
    blk = feat // devices
    me = lax.axis_index("rows")
    turn = LANES // blk
    core, parity = me % 2, (me // turn) % 2

    def swap(array, mask):
        return lax.ppermute(array, "rows", [(i, i ^ mask) for i in range(devices)])

    def rest(number):
        return (number // (2 * turn)) * (turn // 2) + (number % turn) // 2

    place = jnp.stack([core, parity])
    x, w, sums_send, sums_keep, far_send, far_keep, cross = first(
        place, features, coef, labels, passage_id, slot_of, per_owner, blk
    )
    masks = [m for m in range(1, devices) if not m & 1 and not m & turn]
    mine = rest(me)
    far = (far_keep + swap(far_send, 1).astype(F32)).astype(BF16)
    sums = sums_keep + swap(sums_send, 1)
    arrived = swap(far, turn)
    sums_out = sums.astype(BF16)
    sums_in = [swap(sums_out, m) for m in masks]
    near_send, near_keep = second(place, x, w, cross, blk)
    near = near_keep + swap(near_send, 1).astype(F32) + arrived.astype(F32)
    block = lambda n: lax.dynamic_slice_in_dim(near, n * blk, blk, 0)
    hessian = block(mine)
    parts = [swap(block(mine ^ rest(m)).astype(BF16), m) for m in masks]

    for part in sums_in:
        sums = sums + part.astype(F32)
    sums = sums + swap(sums, turn)
    other = swap(sums, 1)
    chip = me // 2
    grad_local = lax.dynamic_slice_in_dim(sums, chip * per_owner, per_owner, 0)
    stack = jnp.concatenate([sums, other], axis=0)
    columns = lax.dynamic_slice_in_dim(stack, me * blk, blk, 1)
    meat = lax.dot_general(
        columns,
        stack,
        (((0,), (0,)), ((), ())),
        precision=lax.Precision.HIGHEST,
        preferred_element_type=F32,
    )
    for part in parts:
        hessian = hessian + part.astype(F32)
    return (hessian, meat, grad_local)


def solution(mesh):
    in_specs = (
        P(("groups", "rows"), None),
        P(),
        P(("groups", "rows")),
        P(("groups", "rows"), None),
        P("groups"),
    )
    out_specs = (
        P(("groups", "rows"), None),
        P(("groups", "rows"), None),
        P(("groups", "rows"), None),
    )
    return jax.shard_map(local, mesh=mesh, in_specs=in_specs, out_specs=out_specs, check_vma=False)
```

```python
import functools

import jax
import jax.numpy as jnp
from jax import lax
from jax.experimental import pallas as pl
from jax.experimental.pallas import tpu as pltpu
from jax.sharding import PartitionSpec as P

BF16 = jnp.bfloat16
F32 = jnp.float32
LANES = 128
VMEM_LIMIT = 28 * 1024 * 1024


def turned_block(x_ref, here, lane, weight):
    return (x_ref[here, pl.ds(lane, LANES)].T.astype(F32) * weight).astype(BF16)


def lane_of(block, parity):
    return pl.multiple_of((2 * block + parity) * LANES, LANES)


def core_rows(blk, core, pairs):
    for pair in range(pairs):
        base = 2 * pair * blk
        yield pl.ds(pair * blk, blk), [
            pl.ds(pl.multiple_of(base + number * blk, 16), blk) for number in (core, 1 - core)
        ]


def first_kernel(
    per_owner, blk, chunks, place, x_hbm, coef_hbm, label_hbm, pid_hbm, slot_hbm,
    x_ref, w_ref, sums_send, sums_keep, send_ref, keep_ref,
    left, send_acc, coef_ref, label_ref, pid_ref, slot_ref, x_sems, sems,
):
    core, parity = place[0], place[1]
    rows, feat = x_ref.shape
    clusters = slot_ref.shape[1]
    half = clusters // 2
    starts = [rows * sum(chunks[:n]) // sum(chunks) for n in range(len(chunks) + 1)]
    spans = [slice(a, b) for a, b in zip(starts, starts[1:])]
    small = [
        pltpu.make_async_copy(source, target, sems.at[n])
        for n, (source, target) in enumerate(
            [(coef_hbm, coef_ref), (slot_hbm, slot_ref), (label_hbm, label_ref), (pid_hbm, pid_ref)]
        )
    ]
    large = [
        pltpu.make_async_copy(x_hbm.at[here], x_ref.at[here], x_sems.at[n])
        for n, here in enumerate(spans)
    ]
    for copy in small:
        copy.start()
    for copy in large:
        copy.start()
    for copy in small:
        copy.wait()
    row = lax.broadcasted_iota(jnp.int32, (clusters, clusters), 0)
    mine = row >= half
    inner = jnp.where(mine, row - half, row)
    slot = (2 * (inner // per_owner) + jnp.where(mine, core, 1 - core)) * per_owner + inner % per_owner
    passage = lax.broadcasted_iota(jnp.int32, (clusters, clusters), 1)
    names = jnp.sum(jnp.where(slot_ref[...] == slot, passage, 0), axis=1, keepdims=True)
    coef = jnp.broadcast_to(coef_ref[...].reshape(1, feat), (16, feat))
    def probabilities(n):
        here = spans[n]
        large[n].wait()
        logits = lax.dot_general(coef, x_ref[here, :], (((1,), (1,)), ((), ())), preferred_element_type=F32)[0:1]
        prob = 1.0 / (1.0 + jnp.exp(-logits))
        return prob * (1.0 - prob), label_ref[:, here].astype(F32) - prob

    def use(n, weight, score):
        here = spans[n]
        w_ref[:, here] = weight
        score = jnp.broadcast_to(score, (LANES, here.stop - here.start)).T
        score = jnp.concatenate([score] * (feat // LANES), axis=1)
        scored = (x_ref[here, :].astype(F32) * score).astype(BF16)
        member = jnp.where(pid_ref[:, here] == names, 1.0, 0.0).astype(BF16)
        sums = jnp.dot(member, scored, preferred_element_type=F32)
        for block in range(feat // (2 * LANES)):
            turned = turned_block(x_ref, here, lane_of(block, 1 - parity), weight)
            for pair in range(LANES // (2 * blk)):
                out = (block * LANES // (2 * blk) + pair) * blk
                for number in range(2):
                    start = out + jnp.where(core == number, 0, feat // 4)
                    at = (2 * pair + number) * blk
                    left[pl.ds(pl.multiple_of(start, 16), blk), here] = turned[at : at + blk]
        add(sums_send, sums[:half], n)
        add(sums_keep, sums[half:], n)

    def add(ref, term, n):
        if n:
            ref[...] += term
        else:
            ref[...] = term

    def multiply(n):
        term = jnp.dot(left[:, spans[n]], x_ref[spans[n], :], preferred_element_type=F32)
        add(keep_ref, term[: feat // 4], n)
        if n < len(spans) - 1:
            add(send_acc, term[feat // 4 :], n)
        else:
            term = term[feat // 4 :]
            send_ref[...] = (term + send_acc[...] if n else term).astype(BF16)

    held = probabilities(0)
    for n in range(len(spans)):
        ahead = probabilities(n + 1) if n + 1 < len(spans) else None
        use(n, *held)
        multiply(n)
        held = ahead


def second_kernel(blk, chunks, place, x_ref, w_ref, far_send, far_keep, send_ref, keep_ref, acc, cross):
    core, parity = place[0], place[1]
    rows, feat = x_ref.shape
    part = rows // chunks
    width = feat // (2 * LANES)
    for packed, (kept, sent) in core_rows(blk, core, feat // (4 * blk)):
        for b in range(width):
            lanes, lane = slice(b * LANES, (b + 1) * LANES), pl.ds(lane_of(b, parity), LANES)
            cross[kept, lanes] = far_keep[packed, lane]
            cross[sent, lanes] = far_send[packed, lane].astype(F32)
    total = None
    for n in range(chunks):
        here = slice(n * part, n * part + part)
        right = jnp.concatenate([x_ref[here, pl.ds(lane_of(b, parity), LANES)] for b in range(width)], axis=1)
        weight = w_ref[:, here]
        left = jnp.concatenate([turned_block(x_ref, here, lane_of(b, parity), weight) for b in range(width)], axis=0)
        term = jnp.dot(left, right, preferred_element_type=F32)
        total = term if total is None else total + term
    turned = cross[...].T
    for b in range(width):
        lanes = slice(b * LANES, (b + 1) * LANES)
        acc[:, pl.ds(lane_of(b, parity), LANES)] = total[:, lanes]
        acc[:, pl.ds(lane_of(b, 1 - parity), LANES)] = turned[:, lanes]
    for packed, (kept, sent) in core_rows(blk, core, feat // (4 * blk)):
        keep_ref[packed, :] = acc[kept, :]
        send_ref[packed, :] = acc[sent, :].astype(BF16)


VMEM_SPEC = pl.BlockSpec(memory_space=pltpu.VMEM)


def first(place, x, coef, labels, pid, slot_of, per_owner, blk, chunks=(1, 2, 5)):
    rows, feat = x.shape
    clusters = slot_of.shape[0]
    hbm = pl.BlockSpec(memory_space=pltpu.HBM)
    shape = jax.ShapeDtypeStruct
    arrays = [x, coef, labels.reshape(1, rows), pid.reshape(1, rows), slot_of.reshape(1, clusters)]
    return pl.pallas_call(
        functools.partial(first_kernel, per_owner, blk, chunks),
        in_specs=[pl.BlockSpec(memory_space=pltpu.SMEM)] + [hbm] * 5,
        out_specs=[VMEM_SPEC] * 6,
        out_shape=[
            shape((rows, feat), BF16),
            shape((1, rows), F32),
            shape((clusters // 2, feat), F32),
            shape((clusters // 2, feat), F32),
            shape((feat // 4, feat), BF16),
            shape((feat // 4, feat), F32),
        ],
        scratch_shapes=[
            pltpu.VMEM((feat // 2, rows), BF16),
            pltpu.VMEM((feat // 4, feat), F32),
            pltpu.VMEM((feat,), BF16),
            pltpu.VMEM((1, rows), jnp.int32),
            pltpu.VMEM((1, rows), jnp.int32),
            pltpu.VMEM((1, clusters), jnp.int32),
            pltpu.SemaphoreType.DMA((len(chunks),)),
            pltpu.SemaphoreType.DMA((4,)),
        ],
        compiler_params=pltpu.CompilerParams(vmem_limit_bytes=VMEM_LIMIT),
        name="scores_and_far",
    )(place, *[pltpu.with_memory_space_constraint(array, pltpu.HBM) for array in arrays])


def second(place, x, w, far_send, far_keep, blk, chunks=4):
    feat = x.shape[1]
    return pl.pallas_call(
        functools.partial(second_kernel, blk, chunks),
        in_specs=[pl.BlockSpec(memory_space=pltpu.SMEM)] + [VMEM_SPEC] * 4,
        out_specs=[VMEM_SPEC] * 2,
        out_shape=[
            jax.ShapeDtypeStruct((feat // 4, feat), BF16),
            jax.ShapeDtypeStruct((feat // 4, feat), F32),
        ],
        scratch_shapes=[pltpu.VMEM((feat // 2, feat), F32), pltpu.VMEM((feat // 2, feat // 2), F32)],
        compiler_params=pltpu.CompilerParams(vmem_limit_bytes=VMEM_LIMIT),
        name="near",
    )(place, x, w, far_send, far_keep)


def local(features, coef, labels, passage_id, slot_of):
    feat = features.shape[1]
    devices = lax.axis_size("rows")
    clusters = slot_of.shape[0]
    per_owner = clusters // devices
    blk = feat // devices
    me = lax.axis_index("rows").astype(jnp.int32)
    turn = LANES // blk
    core, parity = me & 1, (me & turn) // turn

    def swap(array, mask):
        return lax.ppermute(array, "rows", [(i, i ^ mask) for i in range(devices)])

    def rest(number):
        return (number // (2 * turn)) * (turn // 2) + (number % turn) // 2

    place = jnp.stack([core, parity])
    x, w, sums_send, sums_keep, far_send, far_keep = first(
        place, features, coef, labels, passage_id, slot_of, per_owner, blk
    )
    masks = [m for m in range(1, devices) if not m & 1 and not m & turn]
    far_in, sums_in = swap(far_send, 1), swap(sums_send, 1)
    near_send, near_keep = second(place, x, w, far_send, far_keep, blk)
    near_in = swap(near_send, 1)
    far = (far_keep + far_in.astype(F32)).astype(BF16)
    sums = sums_keep + sums_in
    sums_out = sums.astype(BF16)
    arrived = swap(far, turn)
    sums_parts = [swap(sums_out, m) for m in masks]
    near = near_keep + near_in.astype(F32) + arrived.astype(F32)
    block = lambda n: lax.dynamic_slice_in_dim(near, (rest(me) ^ n) * blk, blk, 0)
    hessian = block(0)
    parts = [block(rest(m)).astype(BF16) for m in masks]
    sums_parts, parts = lax.optimization_barrier((sums_parts, parts))
    parts = [swap(part, m) for part, m in zip(parts, masks)]
    for part in sums_parts:
        sums = sums + part.astype(F32)
    sums = sums + swap(sums, turn)
    other = swap(sums, 1)
    chip = me // 2
    grad_local = lax.dynamic_slice_in_dim(sums, chip * per_owner, per_owner, 0)
    stack = jnp.concatenate([sums, other], axis=0)
    columns = lax.dynamic_slice_in_dim(stack, me * blk, blk, 1)
    meat = lax.dot_general(
        columns,
        stack,
        (((0,), (0,)), ((), ())),
        precision=lax.Precision.HIGHEST,
        preferred_element_type=F32,
    )
    for part in parts:
        hessian = hessian + part.astype(F32)
    return (hessian, meat, grad_local)


def solution(mesh):
    in_specs = (
        P(("groups", "rows"), None),
        P(),
        P(("groups", "rows")),
        P(("groups", "rows"), None),
        P("groups"),
    )
    out_specs = (
        P(("groups", "rows"), None),
        P(("groups", "rows"), None),
        P(("groups", "rows"), None),
    )
    return jax.shard_map(local, mesh=mesh, in_specs=in_specs, out_specs=out_specs, check_vma=False)
```

```python
import functools

import jax
import jax.numpy as jnp
from jax import lax
from jax.experimental import pallas as pl
from jax.experimental.pallas import tpu as pltpu
from jax.sharding import PartitionSpec as P

BF16 = jnp.bfloat16
F32 = jnp.float32
LANES = 128
VMEM_LIMIT = 28 * 1024 * 1024


def turned_block(x_ref, here, lane, weight):
    return (x_ref[here, pl.ds(lane, LANES)].T.astype(F32) * weight).astype(BF16)


def lane_of(block, parity):
    return pl.multiple_of((2 * block + parity) * LANES, LANES)


def core_rows(blk, core, pairs):
    for pair in range(pairs):
        base = 2 * pair * blk
        yield pl.ds(pair * blk, blk), [
            pl.ds(pl.multiple_of(base + number * blk, 16), blk) for number in (core, 1 - core)
        ]


def first_kernel(
    per_owner, blk, chunks, place, x_hbm, coef_hbm, label_hbm, pid_hbm, slot_hbm,
    x_ref, w_ref, sums_send, sums_keep, send_ref, keep_ref,
    left, send_acc, coef_ref, label_ref, pid_ref, slot_ref, x_sems, sems,
):
    core, parity = place[0], place[1]
    rows, feat = x_ref.shape
    clusters = slot_ref.shape[1]
    half = clusters // 2
    starts = [rows * sum(chunks[:n]) // sum(chunks) for n in range(len(chunks) + 1)]
    spans = [slice(a, b) for a, b in zip(starts, starts[1:])]
    small = [
        pltpu.make_async_copy(source, target, sems.at[n])
        for n, (source, target) in enumerate(
            [(coef_hbm, coef_ref), (slot_hbm, slot_ref), (label_hbm, label_ref), (pid_hbm, pid_ref)]
        )
    ]
    large = [
        pltpu.make_async_copy(x_hbm.at[here], x_ref.at[here], x_sems.at[n])
        for n, here in enumerate(spans)
    ]
    for copy in small:
        copy.start()
    for copy in large:
        copy.start()
    for copy in small:
        copy.wait()
    row = lax.broadcasted_iota(jnp.int32, (clusters, clusters), 0)
    turn = LANES // blk
    core_of = jnp.where(row >= half, core, 1 - core)
    inner = row % half
    parity_of = jnp.where(inner >= half // 2, parity, 1 - parity)
    inner = inner % (half // 2)
    rest = inner // per_owner
    owner = (rest // (turn // 2)) * (2 * turn) + parity_of * turn + (rest % (turn // 2)) * 2 + core_of
    slot = owner * per_owner + inner % per_owner
    passage = lax.broadcasted_iota(jnp.int32, (clusters, clusters), 1)
    names = jnp.sum(jnp.where(slot_ref[...] == slot, passage, 0), axis=1, keepdims=True)
    coef = jnp.broadcast_to(coef_ref[...].reshape(1, feat), (16, feat))
    def probabilities(n):
        here = spans[n]
        large[n].wait()
        logits = lax.dot_general(coef, x_ref[here, :], (((1,), (1,)), ((), ())), preferred_element_type=F32)[0:1]
        prob = 1.0 / (1.0 + jnp.exp(-logits))
        return prob * (1.0 - prob), label_ref[:, here].astype(F32) - prob

    def use(n, weight, score):
        here = spans[n]
        w_ref[:, here] = weight
        score = jnp.broadcast_to(score, (LANES, here.stop - here.start)).T
        score = jnp.concatenate([score] * (feat // LANES), axis=1)
        scored = (x_ref[here, :].astype(F32) * score).astype(BF16)
        member = jnp.where(pid_ref[:, here] == names, 1.0, 0.0).astype(BF16)
        sums = jnp.dot(member, scored, preferred_element_type=F32)
        for block in range(feat // (2 * LANES)):
            turned = turned_block(x_ref, here, lane_of(block, 1 - parity), weight)
            for pair in range(LANES // (2 * blk)):
                out = (block * LANES // (2 * blk) + pair) * blk
                for number in range(2):
                    start = out + jnp.where(core == number, 0, feat // 4)
                    at = (2 * pair + number) * blk
                    left[pl.ds(pl.multiple_of(start, 16), blk), here] = turned[at : at + blk]
        add(sums_send, sums[:half], n)
        add(sums_keep, sums[half:], n)

    def add(ref, term, n):
        if n:
            ref[...] += term
        else:
            ref[...] = term

    def multiply(n):
        term = jnp.dot(left[:, spans[n]], x_ref[spans[n], :], preferred_element_type=F32)
        add(keep_ref, term[: feat // 4], n)
        if n < len(spans) - 1:
            add(send_acc, term[feat // 4 :], n)
        else:
            term = term[feat // 4 :]
            send_ref[...] = (term + send_acc[...] if n else term).astype(BF16)

    held = probabilities(0)
    for n in range(len(spans)):
        ahead = probabilities(n + 1) if n + 1 < len(spans) else None
        use(n, *held)
        multiply(n)
        held = ahead


def second_kernel(blk, chunks, place, x_ref, w_ref, far_send, far_keep, send_ref, keep_ref, acc, cross):
    core, parity = place[0], place[1]
    rows, feat = x_ref.shape
    part = rows // chunks
    width = feat // (2 * LANES)
    for packed, (kept, sent) in core_rows(blk, core, feat // (4 * blk)):
        for b in range(width):
            lanes, lane = slice(b * LANES, (b + 1) * LANES), pl.ds(lane_of(b, parity), LANES)
            cross[kept, lanes] = far_keep[packed, lane]
            cross[sent, lanes] = far_send[packed, lane].astype(F32)
    total = None
    for n in range(chunks):
        here = slice(n * part, n * part + part)
        right = jnp.concatenate([x_ref[here, pl.ds(lane_of(b, parity), LANES)] for b in range(width)], axis=1)
        weight = w_ref[:, here]
        left = jnp.concatenate([turned_block(x_ref, here, lane_of(b, parity), weight) for b in range(width)], axis=0)
        term = jnp.dot(left, right, preferred_element_type=F32)
        total = term if total is None else total + term
    turned = cross[...].T
    for b in range(width):
        lanes = slice(b * LANES, (b + 1) * LANES)
        acc[:, pl.ds(lane_of(b, parity), LANES)] = total[:, lanes]
        acc[:, pl.ds(lane_of(b, 1 - parity), LANES)] = turned[:, lanes]
    for packed, (kept, sent) in core_rows(blk, core, feat // (4 * blk)):
        keep_ref[packed, :] = acc[kept, :]
        send_ref[packed, :] = acc[sent, :].astype(BF16)


VMEM_SPEC = pl.BlockSpec(memory_space=pltpu.VMEM)


def first(place, x, coef, labels, pid, slot_of, per_owner, blk, chunks=(1, 2, 5)):
    rows, feat = x.shape
    clusters = slot_of.shape[0]
    hbm = pl.BlockSpec(memory_space=pltpu.HBM)
    shape = jax.ShapeDtypeStruct
    arrays = [x, coef, labels.reshape(1, rows), pid.reshape(1, rows), slot_of.reshape(1, clusters)]
    return pl.pallas_call(
        functools.partial(first_kernel, per_owner, blk, chunks),
        in_specs=[pl.BlockSpec(memory_space=pltpu.SMEM)] + [hbm] * 5,
        out_specs=[VMEM_SPEC] * 6,
        out_shape=[
            shape((rows, feat), BF16),
            shape((1, rows), F32),
            shape((clusters // 2, feat), F32),
            shape((clusters // 2, feat), F32),
            shape((feat // 4, feat), BF16),
            shape((feat // 4, feat), F32),
        ],
        scratch_shapes=[
            pltpu.VMEM((feat // 2, rows), BF16),
            pltpu.VMEM((feat // 4, feat), F32),
            pltpu.VMEM((feat,), BF16),
            pltpu.VMEM((1, rows), jnp.int32),
            pltpu.VMEM((1, rows), jnp.int32),
            pltpu.VMEM((1, clusters), jnp.int32),
            pltpu.SemaphoreType.DMA((len(chunks),)),
            pltpu.SemaphoreType.DMA((4,)),
        ],
        compiler_params=pltpu.CompilerParams(vmem_limit_bytes=VMEM_LIMIT),
        name="scores_and_far",
    )(place, *[pltpu.with_memory_space_constraint(array, pltpu.HBM) for array in arrays])


def second(place, x, w, far_send, far_keep, blk, chunks=4):
    feat = x.shape[1]
    return pl.pallas_call(
        functools.partial(second_kernel, blk, chunks),
        in_specs=[pl.BlockSpec(memory_space=pltpu.SMEM)] + [VMEM_SPEC] * 4,
        out_specs=[VMEM_SPEC] * 2,
        out_shape=[
            jax.ShapeDtypeStruct((feat // 4, feat), BF16),
            jax.ShapeDtypeStruct((feat // 4, feat), F32),
        ],
        scratch_shapes=[pltpu.VMEM((feat // 2, feat), F32), pltpu.VMEM((feat // 2, feat // 2), F32)],
        compiler_params=pltpu.CompilerParams(vmem_limit_bytes=VMEM_LIMIT),
        name="near",
    )(place, x, w, far_send, far_keep)


def local(features, coef, labels, passage_id, slot_of):
    feat = features.shape[1]
    devices = lax.axis_size("rows")
    clusters = slot_of.shape[0]
    per_owner = clusters // devices
    blk = feat // devices
    me = lax.axis_index("rows").astype(jnp.int32)
    turn = LANES // blk
    core, parity = me & 1, (me & turn) // turn

    def swap(array, mask):
        return lax.ppermute(array, "rows", [(i, i ^ mask) for i in range(devices)])

    def rest(number):
        return (number // (2 * turn)) * (turn // 2) + (number % turn) // 2

    place = jnp.stack([core, parity])
    x, w, sums_send, sums_keep, far_send, far_keep = first(
        place, features, coef, labels, passage_id, slot_of, per_owner, blk
    )
    masks = [m for m in range(1, devices) if not m & 1 and not m & turn]
    far_in, sums_in = swap(far_send, 1), swap(sums_send, 1)
    near_send, near_keep = second(place, x, w, far_send, far_keep, blk)
    near_in = swap(near_send, 1)
    far = (far_keep + far_in.astype(F32)).astype(BF16)
    sums_keep, _ = lax.optimization_barrier((sums_keep, near_keep))
    sums = sums_keep + sums_in
    quarter = clusters // 4
    sums_far, sums_near = sums[:quarter], sums[quarter:]
    sums = sums_near + swap(sums_far.astype(BF16), turn).astype(F32)
    arrived = swap(far, turn)
    sums_out = sums.astype(BF16)
    sums_parts = [swap(sums_out, m) for m in masks]
    near = near_keep + near_in.astype(F32) + arrived.astype(F32)
    block = lambda n: lax.dynamic_slice_in_dim(near, (rest(me) ^ n) * blk, blk, 0)
    hessian = block(0)
    parts = [block(rest(m)).astype(BF16) for m in masks]
    for part in sums_parts:
        sums = sums + part.astype(F32)
    sums, parts = lax.optimization_barrier((sums, parts))
    parts = [swap(part, m) for part, m in zip(parts, masks)]
    grad_local = lax.dynamic_slice_in_dim(sums, rest(me) * per_owner, per_owner, 0)
    sums = jnp.concatenate([sums, swap(sums, turn)], axis=0)
    stack = jnp.concatenate([sums, swap(sums, 1)], axis=0)
    columns = lax.dynamic_slice_in_dim(stack, me * blk, blk, 1)
    meat = lax.dot_general(
        columns,
        stack,
        (((0,), (0,)), ((), ())),
        precision=lax.Precision.HIGHEST,
        preferred_element_type=F32,
    )
    parts, meat = lax.optimization_barrier((parts, meat))
    for part in parts:
        hessian = hessian + part.astype(F32)
    return (hessian, meat, grad_local)


def solution(mesh):
    in_specs = (
        P(("groups", "rows"), None),
        P(),
        P(("groups", "rows")),
        P(("groups", "rows"), None),
        P("groups"),
    )
    out_specs = (
        P(("groups", "rows"), None),
        P(("groups", "rows"), None),
        P(("groups", "rows"), None),
    )
    return jax.shard_map(local, mesh=mesh, in_specs=in_specs, out_specs=out_specs, check_vma=False)
```

```python
import functools

import jax
import jax.numpy as jnp
from jax import lax
from jax.experimental import pallas as pl
from jax.experimental.pallas import tpu as pltpu
from jax.sharding import PartitionSpec as P

BF16 = jnp.bfloat16
F32 = jnp.float32
LANES = 128
VMEM_LIMIT = 20 * 1024 * 1024


def turned_block(x_ref, here, lane, weight):
    return (x_ref[here, pl.ds(lane, LANES)].T.astype(F32) * weight).astype(BF16)


def lane_of(block, parity):
    return pl.multiple_of((2 * block + parity) * LANES, LANES)


def core_rows(blk, core, pairs):
    for pair in range(pairs):
        base = 2 * pair * blk
        yield pl.ds(pair * blk, blk), [
            pl.ds(pl.multiple_of(base + number * blk, 16), blk) for number in (core, 1 - core)
        ]


def first_kernel(
    per_owner, blk, chunks, place, x_hbm, coef_hbm, label_hbm, pid_hbm, slot_hbm,
    x_ref, w_ref, sums_send, sums_keep, send_ref, keep_ref,
    left, send_acc, coef_ref, label_ref, pid_ref, slot_ref, x_sems, sems,
):
    core, parity = place[0], place[1]
    rows, feat = x_ref.shape
    clusters = slot_ref.shape[1]
    half = clusters // 2
    starts = [rows * sum(chunks[:n]) // sum(chunks) for n in range(len(chunks) + 1)]
    spans = [slice(a, b) for a, b in zip(starts, starts[1:])]
    small = [
        pltpu.make_async_copy(source, target, sems.at[n])
        for n, (source, target) in enumerate(
            [(coef_hbm, coef_ref), (slot_hbm, slot_ref), (label_hbm, label_ref), (pid_hbm, pid_ref)]
        )
    ]
    large = [
        pltpu.make_async_copy(x_hbm.at[here], x_ref.at[here], x_sems.at[n])
        for n, here in enumerate(spans)
    ]
    for copy in small:
        copy.start()
    for copy in large:
        copy.start()
    for copy in small:
        copy.wait()
    row = lax.broadcasted_iota(jnp.int32, (clusters, clusters), 0)
    turn = LANES // blk
    core_of = jnp.where(row >= half, core, 1 - core)
    inner = row % half
    parity_of = jnp.where(inner >= half // 2, parity, 1 - parity)
    inner = inner % (half // 2)
    rest = inner // per_owner
    owner = (rest // (turn // 2)) * (2 * turn) + parity_of * turn + (rest % (turn // 2)) * 2 + core_of
    slot = owner * per_owner + inner % per_owner
    passage = lax.broadcasted_iota(jnp.int32, (clusters, clusters), 1)
    names = jnp.sum(jnp.where(slot_ref[...] == slot, passage, 0), axis=1, keepdims=True)
    coef = jnp.broadcast_to(coef_ref[...].reshape(1, feat), (16, feat))
    def probabilities(n):
        here = spans[n]
        large[n].wait()
        logits = lax.dot_general(coef, x_ref[here, :], (((1,), (1,)), ((), ())), preferred_element_type=F32)[0:1]
        prob = 1.0 / (1.0 + jnp.exp(-logits))
        return prob * (1.0 - prob), label_ref[:, here].astype(F32) - prob

    def use(n, weight, score):
        here = spans[n]
        w_ref[:, here] = weight
        score = jnp.broadcast_to(score, (LANES, here.stop - here.start)).T
        score = jnp.concatenate([score] * (feat // LANES), axis=1)
        scored = (x_ref[here, :].astype(F32) * score).astype(BF16)
        member = jnp.where(pid_ref[:, here] == names, 1.0, 0.0).astype(BF16)
        sums = jnp.dot(member, scored, preferred_element_type=F32)
        for block in range(feat // (2 * LANES)):
            turned = turned_block(x_ref, here, lane_of(block, 1 - parity), weight)
            for pair in range(LANES // (2 * blk)):
                out = (block * LANES // (2 * blk) + pair) * blk
                for number in range(2):
                    start = out + jnp.where(core == number, 0, feat // 4)
                    at = (2 * pair + number) * blk
                    left[pl.ds(pl.multiple_of(start, 16), blk), here] = turned[at : at + blk]
        add(sums_send, sums[:half], n)
        add(sums_keep, sums[half:], n)

    def add(ref, term, n):
        if n:
            ref[...] += term
        else:
            ref[...] = term

    def multiply(n):
        term = jnp.dot(left[:, spans[n]], x_ref[spans[n], :], preferred_element_type=F32)
        add(keep_ref, term[: feat // 4], n)
        if n < len(spans) - 1:
            add(send_acc, term[feat // 4 :], n)
        else:
            term = term[feat // 4 :]
            send_ref[...] = (term + send_acc[...] if n else term).astype(BF16)

    held = probabilities(0)
    for n in range(len(spans)):
        ahead = probabilities(n + 1) if n + 1 < len(spans) else None
        use(n, *held)
        multiply(n)
        held = ahead


def second_kernel(blk, chunks, place, x_ref, w_ref, far_send, far_keep, send_ref, keep_ref, acc, cross):
    core, parity = place[0], place[1]
    rows, feat = x_ref.shape
    part = rows // chunks
    width = feat // (2 * LANES)
    for packed, (kept, sent) in core_rows(blk, core, feat // (4 * blk)):
        for b in range(width):
            lanes, lane = slice(b * LANES, (b + 1) * LANES), pl.ds(lane_of(b, parity), LANES)
            cross[kept, lanes] = far_keep[packed, lane]
            cross[sent, lanes] = far_send[packed, lane].astype(F32)
    total = corner = None
    middle = width * LANES // 2
    for n in range(chunks):
        here = slice(n * part, n * part + part)
        right = jnp.concatenate([x_ref[here, pl.ds(lane_of(b, parity), LANES)] for b in range(width)], axis=1)
        weight = w_ref[:, here]
        left = jnp.concatenate([turned_block(x_ref, here, lane_of(b, parity), weight) for b in range(width)], axis=0)
        term = jnp.dot(left[:middle], right, preferred_element_type=F32)
        total = term if total is None else total + term
        term = jnp.dot(left[middle:], right[:, middle:], preferred_element_type=F32)
        corner = term if corner is None else corner + term
    corner = jnp.concatenate([total[:, middle:].T, corner], axis=1)
    total = jnp.concatenate([total, corner], axis=0)
    turned = cross[...].T
    for b in range(width):
        lanes = slice(b * LANES, (b + 1) * LANES)
        acc[:, pl.ds(lane_of(b, parity), LANES)] = total[:, lanes]
        acc[:, pl.ds(lane_of(b, 1 - parity), LANES)] = turned[:, lanes]
    for packed, (kept, sent) in core_rows(blk, core, feat // (4 * blk)):
        keep_ref[packed, :] = acc[kept, :]
        send_ref[packed, :] = acc[sent, :].astype(BF16)


VMEM_SPEC = pl.BlockSpec(memory_space=pltpu.VMEM)


def first(place, x, coef, labels, pid, slot_of, per_owner, blk, chunks=(1, 2, 5)):
    rows, feat = x.shape
    clusters = slot_of.shape[0]
    hbm = pl.BlockSpec(memory_space=pltpu.HBM)
    shape = jax.ShapeDtypeStruct
    arrays = [x, coef, labels.reshape(1, rows), pid.reshape(1, rows), slot_of.reshape(1, clusters)]
    return pl.pallas_call(
        functools.partial(first_kernel, per_owner, blk, chunks),
        in_specs=[pl.BlockSpec(memory_space=pltpu.SMEM)] + [hbm] * 5,
        out_specs=[VMEM_SPEC] * 6,
        out_shape=[
            shape((rows, feat), BF16),
            shape((1, rows), F32),
            shape((clusters // 2, feat), F32),
            shape((clusters // 2, feat), F32),
            shape((feat // 4, feat), BF16),
            shape((feat // 4, feat), F32),
        ],
        scratch_shapes=[
            pltpu.VMEM((feat // 2, rows), BF16),
            pltpu.VMEM((feat // 4, feat), F32),
            pltpu.VMEM((feat,), BF16),
            pltpu.VMEM((1, rows), jnp.int32),
            pltpu.VMEM((1, rows), jnp.int32),
            pltpu.VMEM((1, clusters), jnp.int32),
            pltpu.SemaphoreType.DMA((len(chunks),)),
            pltpu.SemaphoreType.DMA((4,)),
        ],
        compiler_params=pltpu.CompilerParams(vmem_limit_bytes=VMEM_LIMIT),
        name="scores_and_far",
    )(place, *[pltpu.with_memory_space_constraint(array, pltpu.HBM) for array in arrays])


def second(place, x, w, far_send, far_keep, blk, chunks=4):
    feat = x.shape[1]
    return pl.pallas_call(
        functools.partial(second_kernel, blk, chunks),
        in_specs=[pl.BlockSpec(memory_space=pltpu.SMEM)] + [VMEM_SPEC] * 4,
        out_specs=[VMEM_SPEC] * 2,
        out_shape=[
            jax.ShapeDtypeStruct((feat // 4, feat), BF16),
            jax.ShapeDtypeStruct((feat // 4, feat), F32),
        ],
        scratch_shapes=[pltpu.VMEM((feat // 2, feat), F32), pltpu.VMEM((feat // 2, feat // 2), F32)],
        compiler_params=pltpu.CompilerParams(vmem_limit_bytes=VMEM_LIMIT),
        name="near",
    )(place, x, w, far_send, far_keep)


def local(features, coef, labels, passage_id, slot_of):
    feat = features.shape[1]
    devices = lax.axis_size("rows")
    clusters = slot_of.shape[0]
    per_owner = clusters // devices
    blk = feat // devices
    me = lax.axis_index("rows").astype(jnp.int32)
    turn = LANES // blk
    core, parity = me & 1, (me & turn) // turn

    def swap(array, mask):
        return lax.ppermute(array, "rows", [(i, i ^ mask) for i in range(devices)])

    def rest(number):
        return (number // (2 * turn)) * (turn // 2) + (number % turn) // 2

    place = jnp.stack([core, parity])
    x, w, sums_send, sums_keep, far_send, far_keep = first(
        place, features, coef, labels, passage_id, slot_of, per_owner, blk
    )
    masks = [m for m in range(1, devices) if not m & 1 and not m & turn]
    masks = masks[1:] + masks[:1]
    far_in, sums_in = swap(far_send, 1), swap(sums_send, 1)
    near_send, near_keep = second(place, x, w, far_send, far_keep, blk)
    near_in = swap(near_send, 1)
    far = (far_keep + far_in.astype(F32)).astype(BF16)
    sums_keep, _ = lax.optimization_barrier((sums_keep, near_keep))
    sums = sums_keep + sums_in
    quarter = clusters // 4
    sums_far, sums_near = sums[:quarter], sums[quarter:]
    sums = sums_near + swap(sums_far.astype(BF16), turn).astype(F32)
    arrived = swap(far, turn)
    sums_out = sums.astype(BF16)
    sums_parts = [swap(sums_out, m) for m in masks]
    near = near_keep + near_in.astype(F32) + arrived.astype(F32)
    block = lambda n: lax.dynamic_slice_in_dim(near, (rest(me) ^ n) * blk, blk, 0)
    hessian = block(0)
    parts = [block(rest(m)).astype(BF16) for m in masks]
    for part in sums_parts:
        sums = sums + part.astype(F32)
    sums, parts = lax.optimization_barrier((sums, parts))
    parts = [swap(part, m) for part, m in zip(parts, masks)]
    grad_local = lax.dynamic_slice_in_dim(sums, rest(me) * per_owner, per_owner, 0)
    sums = jnp.concatenate([sums, swap(sums, turn)], axis=0)
    stack = jnp.concatenate([sums, swap(sums, 1)], axis=0)
    columns = lax.dynamic_slice_in_dim(stack, me * blk, blk, 1)
    meat = lax.dot_general(
        columns,
        stack,
        (((0,), (0,)), ((), ())),
        precision=lax.Precision.HIGHEST,
        preferred_element_type=F32,
    )
    parts, meat = lax.optimization_barrier((parts, meat))
    for part in parts:
        hessian = hessian + part.astype(F32)
    return (hessian, meat, grad_local)


def solution(mesh):
    in_specs = (
        P(("groups", "rows"), None),
        P(),
        P(("groups", "rows")),
        P(("groups", "rows"), None),
        P("groups"),
    )
    out_specs = (
        P(("groups", "rows"), None),
        P(("groups", "rows"), None),
        P(("groups", "rows"), None),
    )
    return jax.shard_map(local, mesh=mesh, in_specs=in_specs, out_specs=out_specs, check_vma=False)
```

```python
import functools

import jax
import jax.numpy as jnp
from jax import lax
from jax.experimental import pallas as pl
from jax.experimental.pallas import tpu as pltpu
from jax.sharding import PartitionSpec as P

BF16 = jnp.bfloat16
F32 = jnp.float32
LANES = 128
VMEM_LIMIT = 20 * 1024 * 1024


def turned_block(x_ref, here, lane, weight):
    return (x_ref[here, pl.ds(lane, LANES)].T.astype(F32) * weight).astype(BF16)


def lane_of(block, parity):
    return pl.multiple_of((2 * block + parity) * LANES, LANES)


def core_rows(blk, core, pairs):
    for pair in range(pairs):
        base = 2 * pair * blk
        yield pl.ds(pair * blk, blk), [
            pl.ds(pl.multiple_of(base + number * blk, 16), blk) for number in (core, 1 - core)
        ]


def first_kernel(
    per_owner, blk, chunks, place, x_hbm, coef_hbm, label_hbm, pid_hbm, slot_hbm,
    x_ref, w_ref, sums_send, sums_keep, send_ref, keep_ref,
    left, send_acc, coef_ref, label_ref, pid_ref, slot_ref, x_sems, sems,
):
    core, parity = place[0], place[1]
    rows, feat = x_ref.shape
    clusters = slot_ref.shape[1]
    half = clusters // 2
    starts = [rows * sum(chunks[:n]) // sum(chunks) for n in range(len(chunks) + 1)]
    spans = [slice(a, b) for a, b in zip(starts, starts[1:])]
    small = [
        pltpu.make_async_copy(source, target, sems.at[n])
        for n, (source, target) in enumerate(
            [(coef_hbm, coef_ref), (slot_hbm, slot_ref), (label_hbm, label_ref), (pid_hbm, pid_ref)]
        )
    ]
    large = [
        pltpu.make_async_copy(x_hbm.at[here], x_ref.at[here], x_sems.at[n])
        for n, here in enumerate(spans)
    ]
    for copy in small:
        copy.start()
    for copy in large:
        copy.start()
    for copy in small:
        copy.wait()
    row = lax.broadcasted_iota(jnp.int32, (clusters, clusters), 0)
    turn = LANES // blk
    core_of = jnp.where(row >= half, core, 1 - core)
    inner = row % half
    parity_of = jnp.where(inner >= half // 2, parity, 1 - parity)
    inner = inner % (half // 2)
    rest = inner // per_owner
    owner = (rest // (turn // 2)) * (2 * turn) + parity_of * turn + (rest % (turn // 2)) * 2 + core_of
    slot = owner * per_owner + inner % per_owner
    passage = lax.broadcasted_iota(jnp.int32, (clusters, clusters), 1)
    names = jnp.sum(jnp.where(slot_ref[...] == slot, passage, 0), axis=1, keepdims=True)
    coef = jnp.broadcast_to(coef_ref[...].reshape(1, feat), (16, feat))
    def probabilities(n):
        here = spans[n]
        large[n].wait()
        logits = lax.dot_general(coef, x_ref[here, :], (((1,), (1,)), ((), ())), preferred_element_type=F32)[0:1]
        prob = 1.0 / (1.0 + jnp.exp(-logits))
        return prob * (1.0 - prob), label_ref[:, here].astype(F32) - prob

    def use(n, weight, score):
        here = spans[n]
        w_ref[:, here] = weight
        score = jnp.broadcast_to(score, (LANES, here.stop - here.start)).T
        score = jnp.concatenate([score] * (feat // LANES), axis=1)
        scored = (x_ref[here, :].astype(F32) * score).astype(BF16)
        member = jnp.where(pid_ref[:, here] == names, 1.0, 0.0).astype(BF16)
        sums = jnp.dot(member, scored, preferred_element_type=F32)
        for block in range(feat // (2 * LANES)):
            turned = turned_block(x_ref, here, lane_of(block, 1 - parity), weight)
            for pair in range(LANES // (2 * blk)):
                out = (block * LANES // (2 * blk) + pair) * blk
                for number in range(2):
                    start = out + jnp.where(core == number, 0, feat // 4)
                    at = (2 * pair + number) * blk
                    left[pl.ds(pl.multiple_of(start, 16), blk), here] = turned[at : at + blk]
        add(sums_send, sums[:half], n)
        add(sums_keep, sums[half:], n)

    def add(ref, term, n):
        if n:
            ref[...] += term
        else:
            ref[...] = term

    def multiply(n):
        term = jnp.dot(left[:, spans[n]], x_ref[spans[n], :], preferred_element_type=F32)
        add(keep_ref, term[: feat // 4], n)
        if n < len(spans) - 1:
            add(send_acc, term[feat // 4 :], n)
        else:
            term = term[feat // 4 :]
            send_ref[...] = (term + send_acc[...] if n else term).astype(BF16)

    held = probabilities(0)
    for n in range(len(spans)):
        ahead = probabilities(n + 1) if n + 1 < len(spans) else None
        use(n, *held)
        multiply(n)
        held = ahead


def second_kernel(blk, chunks, place, x_ref, w_ref, far_send, far_keep, send_ref, keep_ref, acc, cross):
    core, parity = place[0], place[1]
    rows, feat = x_ref.shape
    part = rows // chunks
    width = feat // (2 * LANES)
    for packed, (kept, sent) in core_rows(blk, core, feat // (4 * blk)):
        for b in range(width):
            lanes, lane = slice(b * LANES, (b + 1) * LANES), pl.ds(lane_of(b, parity), LANES)
            cross[kept, lanes] = far_keep[packed, lane]
            cross[sent, lanes] = far_send[packed, lane].astype(F32)
    total = corner = None
    middle = width * LANES // 2
    for n in range(chunks):
        here = slice(n * part, n * part + part)
        right = jnp.concatenate([x_ref[here, pl.ds(lane_of(b, parity), LANES)] for b in range(width)], axis=1)
        weight = w_ref[:, here]
        left = jnp.concatenate([turned_block(x_ref, here, lane_of(b, parity), weight) for b in range(width)], axis=0)
        term = jnp.dot(left[:middle], right, preferred_element_type=F32)
        total = term if total is None else total + term
        term = jnp.dot(left[middle:], right[:, middle:], preferred_element_type=F32)
        corner = term if corner is None else corner + term
    corner = jnp.concatenate([total[:, middle:].T, corner], axis=1)
    total = jnp.concatenate([total, corner], axis=0)
    turned = cross[...].T
    for b in range(width):
        lanes = slice(b * LANES, (b + 1) * LANES)
        acc[:, pl.ds(lane_of(b, parity), LANES)] = total[:, lanes]
        acc[:, pl.ds(lane_of(b, 1 - parity), LANES)] = turned[:, lanes]
    for packed, (kept, sent) in core_rows(blk, core, feat // (4 * blk)):
        keep_ref[packed, :] = acc[kept, :]
        send_ref[packed, :] = acc[sent, :].astype(BF16)


VMEM_SPEC = pl.BlockSpec(memory_space=pltpu.VMEM)


def first(place, x, coef, labels, pid, slot_of, per_owner, blk, chunks=(1, 2, 5)):
    rows, feat = x.shape
    clusters = slot_of.shape[0]
    hbm = pl.BlockSpec(memory_space=pltpu.HBM)
    shape = jax.ShapeDtypeStruct
    arrays = [x, coef, labels.reshape(1, rows), pid.reshape(1, rows), slot_of.reshape(1, clusters)]
    return pl.pallas_call(
        functools.partial(first_kernel, per_owner, blk, chunks),
        in_specs=[pl.BlockSpec(memory_space=pltpu.SMEM)] + [hbm] * 5,
        out_specs=[VMEM_SPEC] * 6,
        out_shape=[
            shape((rows, feat), BF16),
            shape((1, rows), F32),
            shape((clusters // 2, feat), F32),
            shape((clusters // 2, feat), F32),
            shape((feat // 4, feat), BF16),
            shape((feat // 4, feat), F32),
        ],
        scratch_shapes=[
            pltpu.VMEM((feat // 2, rows), BF16),
            pltpu.VMEM((feat // 4, feat), F32),
            pltpu.VMEM((feat,), BF16),
            pltpu.VMEM((1, rows), jnp.int32),
            pltpu.VMEM((1, rows), jnp.int32),
            pltpu.VMEM((1, clusters), jnp.int32),
            pltpu.SemaphoreType.DMA((len(chunks),)),
            pltpu.SemaphoreType.DMA((4,)),
        ],
        compiler_params=pltpu.CompilerParams(vmem_limit_bytes=VMEM_LIMIT),
        name="scores_and_far",
    )(place, *[pltpu.with_memory_space_constraint(array, pltpu.HBM) for array in arrays])


def second(place, x, w, far_send, far_keep, blk, chunks=4):
    feat = x.shape[1]
    return pl.pallas_call(
        functools.partial(second_kernel, blk, chunks),
        in_specs=[pl.BlockSpec(memory_space=pltpu.SMEM)] + [VMEM_SPEC] * 4,
        out_specs=[VMEM_SPEC] * 2,
        out_shape=[
            jax.ShapeDtypeStruct((feat // 4, feat), BF16),
            jax.ShapeDtypeStruct((feat // 4, feat), F32),
        ],
        scratch_shapes=[pltpu.VMEM((feat // 2, feat), F32), pltpu.VMEM((feat // 2, feat // 2), F32)],
        compiler_params=pltpu.CompilerParams(vmem_limit_bytes=VMEM_LIMIT),
        name="near",
    )(place, x, w, far_send, far_keep)


def local(features, coef, labels, passage_id, slot_of):
    feat = features.shape[1]
    devices = lax.axis_size("rows")
    clusters = slot_of.shape[0]
    per_owner = clusters // devices
    blk = feat // devices
    me = lax.axis_index("rows").astype(jnp.int32)
    turn = LANES // blk
    core, parity = me & 1, (me & turn) // turn

    def swap(array, mask):
        return lax.ppermute(array, "rows", [(i, i ^ mask) for i in range(devices)])

    def rest(number):
        return (number // (2 * turn)) * (turn // 2) + (number % turn) // 2

    place = jnp.stack([core, parity])
    x, w, sums_send, sums_keep, far_send, far_keep = first(
        place, features, coef, labels, passage_id, slot_of, per_owner, blk
    )
    masks = [m for m in range(1, devices) if not m & 1 and not m & turn]
    masks = masks[1:] + masks[:1]
    far_in, sums_in = swap(far_send, 1), swap(sums_send, 1)
    far = (far_keep + far_in.astype(F32)).astype(BF16)
    sums = sums_keep + sums_in
    quarter = clusters // 4
    sums_far, sums_near = sums[:quarter].astype(BF16), sums[quarter:]
    w, _ = lax.optimization_barrier((w, (far, sums_far)))
    near_send, near_keep = second(place, x, w, far_send, far_keep, blk)
    near_in = swap(near_send, 1)
    sums = sums_near + swap(sums_far, turn).astype(F32)
    arrived = swap(far, turn)
    sums_out = sums.astype(BF16)
    sums_parts = [swap(sums_out, m) for m in sorted(masks)]
    near = near_keep + near_in.astype(F32) + arrived.astype(F32)
    block = lambda n: lax.dynamic_slice_in_dim(near, (rest(me) ^ n) * blk, blk, 0)
    hessian = block(0)
    parts = [block(rest(m)).astype(BF16) for m in masks]
    for part in sums_parts:
        sums = sums + part.astype(F32)
    sums, parts = lax.optimization_barrier((sums, parts))
    parts = [swap(part, m) for part, m in zip(parts, masks)]
    grad_local = lax.dynamic_slice_in_dim(sums, rest(me) * per_owner, per_owner, 0)
    sums = jnp.concatenate([sums, swap(sums, turn)], axis=0)
    stack = jnp.concatenate([sums, swap(sums, 1)], axis=0)
    columns = lax.dynamic_slice_in_dim(stack, me * blk, blk, 1)
    meat = lax.dot_general(
        columns,
        stack,
        (((0,), (0,)), ((), ())),
        precision=lax.Precision.HIGHEST,
        preferred_element_type=F32,
    )
    parts, meat = lax.optimization_barrier((parts, meat))
    for part in parts:
        hessian = hessian + part.astype(F32)
    return (hessian, meat, grad_local)


def solution(mesh):
    in_specs = (
        P(("groups", "rows"), None),
        P(),
        P(("groups", "rows")),
        P(("groups", "rows"), None),
        P("groups"),
    )
    out_specs = (
        P(("groups", "rows"), None),
        P(("groups", "rows"), None),
        P(("groups", "rows"), None),
    )
    return jax.shard_map(local, mesh=mesh, in_specs=in_specs, out_specs=out_specs, check_vma=False)
```

```python
import functools

import jax
import jax.numpy as jnp
from jax import lax
from jax.experimental import pallas as pl
from jax.experimental.pallas import tpu as pltpu
from jax.sharding import PartitionSpec as P

BF16 = jnp.bfloat16
F32 = jnp.float32
LANES = 128
VMEM_LIMIT = 20 * 1024 * 1024


def turned_block(x_ref, here, lane, weight):
    return (x_ref[here, pl.ds(lane, LANES)].T.astype(F32) * weight).astype(BF16)


def lane_of(block, parity):
    return pl.multiple_of((2 * block + parity) * LANES, LANES)


def core_rows(blk, core, pairs):
    for pair in range(pairs):
        base = 2 * pair * blk
        yield pl.ds(pair * blk, blk), [
            pl.ds(pl.multiple_of(base + number * blk, 16), blk) for number in (core, 1 - core)
        ]


def first_kernel(
    per_owner, blk, chunks, place, x_hbm, coef_hbm, label_hbm, pid_hbm, slot_hbm,
    x_ref, w_ref, sums_send, sums_keep, send_ref, keep_ref,
    left, send_acc, coef_ref, label_ref, pid_ref, slot_ref, x_sems, sems,
):
    core, parity = place[0], place[1]
    rows, feat = x_ref.shape
    clusters = slot_ref.shape[1]
    half = clusters // 2
    starts = [rows * sum(chunks[:n]) // sum(chunks) for n in range(len(chunks) + 1)]
    spans = [slice(a, b) for a, b in zip(starts, starts[1:])]
    small = [
        pltpu.make_async_copy(source, target, sems.at[n])
        for n, (source, target) in enumerate(
            [(coef_hbm, coef_ref), (slot_hbm, slot_ref), (label_hbm, label_ref), (pid_hbm, pid_ref)]
        )
    ]
    large = [
        pltpu.make_async_copy(x_hbm.at[here], x_ref.at[here], x_sems.at[n])
        for n, here in enumerate(spans)
    ]
    for copy in small:
        copy.start()
    for copy in large:
        copy.start()
    for copy in small:
        copy.wait()
    row = lax.broadcasted_iota(jnp.int32, (clusters, clusters), 0)
    turn = LANES // blk
    core_of = jnp.where(row >= half, core, 1 - core)
    inner = row % half
    parity_of = jnp.where(inner >= half // 2, parity, 1 - parity)
    inner = inner % (half // 2)
    rest = inner // per_owner
    owner = (rest // (turn // 2)) * (2 * turn) + parity_of * turn + (rest % (turn // 2)) * 2 + core_of
    slot = owner * per_owner + inner % per_owner
    passage = lax.broadcasted_iota(jnp.int32, (clusters, clusters), 1)
    names = jnp.sum(jnp.where(slot_ref[...] == slot, passage, 0), axis=1, keepdims=True)
    coef = jnp.broadcast_to(coef_ref[...].reshape(1, feat), (16, feat))
    def probabilities(n):
        here = spans[n]
        large[n].wait()
        logits = lax.dot_general(coef, x_ref[here, :], (((1,), (1,)), ((), ())), preferred_element_type=F32)[0:1]
        prob = 1.0 / (1.0 + jnp.exp(-logits))
        return prob * (1.0 - prob), label_ref[:, here].astype(F32) - prob

    def use(n, weight, score):
        here = spans[n]
        w_ref[:, here] = weight
        score = jnp.broadcast_to(score, (LANES, here.stop - here.start)).T
        score = jnp.concatenate([score] * (feat // LANES), axis=1)
        scored = (x_ref[here, :].astype(F32) * score).astype(BF16)
        member = jnp.where(pid_ref[:, here] == names, 1.0, 0.0).astype(BF16)
        sums = jnp.dot(member, scored, preferred_element_type=F32)
        for block in range(feat // (2 * LANES)):
            turned = turned_block(x_ref, here, lane_of(block, 1 - parity), weight)
            for pair in range(LANES // (2 * blk)):
                out = (block * LANES // (2 * blk) + pair) * blk
                for number in range(2):
                    start = out + jnp.where(core == number, 0, feat // 4)
                    at = (2 * pair + number) * blk
                    left[pl.ds(pl.multiple_of(start, 16), blk), here] = turned[at : at + blk]
        add(sums_send, sums[:half], n)
        add(sums_keep, sums[half:], n)

    def add(ref, term, n):
        if n:
            ref[...] += term
        else:
            ref[...] = term

    def multiply(n):
        term = jnp.dot(left[:, spans[n]], x_ref[spans[n], :], preferred_element_type=F32)
        add(keep_ref, term[: feat // 4], n)
        if n < len(spans) - 1:
            add(send_acc, term[feat // 4 :], n)
        else:
            term = term[feat // 4 :]
            send_ref[...] = (term + send_acc[...] if n else term).astype(BF16)

    held = probabilities(0)
    for n in range(len(spans)):
        ahead = probabilities(n + 1) if n + 1 < len(spans) else None
        use(n, *held)
        multiply(n)
        held = ahead


def second_kernel(blk, chunks, place, x_ref, w_ref, far_send, far_keep, send_ref, keep_ref, acc, cross):
    core, parity = place[0], place[1]
    rows, feat = x_ref.shape
    part = rows // chunks
    width = feat // (2 * LANES)
    for packed, (kept, sent) in core_rows(blk, core, feat // (4 * blk)):
        for b in range(width):
            lanes, lane = slice(b * LANES, (b + 1) * LANES), pl.ds(lane_of(b, parity), LANES)
            cross[kept, lanes] = far_keep[packed, lane]
            cross[sent, lanes] = far_send[packed, lane].astype(F32)
    total = corner = None
    middle = width * LANES // 2
    for n in range(chunks):
        here = slice(n * part, n * part + part)
        right = jnp.concatenate([x_ref[here, pl.ds(lane_of(b, parity), LANES)] for b in range(width)], axis=1)
        weight = w_ref[:, here]
        left = jnp.concatenate([turned_block(x_ref, here, lane_of(b, parity), weight) for b in range(width)], axis=0)
        term = jnp.dot(left[:middle], right, preferred_element_type=F32)
        total = term if total is None else total + term
        term = jnp.dot(left[middle:], right[:, middle:], preferred_element_type=F32)
        corner = term if corner is None else corner + term
    corner = jnp.concatenate([total[:, middle:].T, corner], axis=1)
    total = jnp.concatenate([total, corner], axis=0)
    turned = cross[...].T
    for b in range(width):
        lanes = slice(b * LANES, (b + 1) * LANES)
        acc[:, pl.ds(lane_of(b, parity), LANES)] = total[:, lanes]
        acc[:, pl.ds(lane_of(b, 1 - parity), LANES)] = turned[:, lanes]
    for packed, (kept, sent) in core_rows(blk, core, feat // (4 * blk)):
        keep_ref[packed, :] = acc[kept, :]
        send_ref[packed, :] = acc[sent, :].astype(BF16)


VMEM_SPEC = pl.BlockSpec(memory_space=pltpu.VMEM)


def first(place, x, coef, labels, pid, slot_of, per_owner, blk, chunks=(1, 2, 5)):
    rows, feat = x.shape
    clusters = slot_of.shape[0]
    hbm = pl.BlockSpec(memory_space=pltpu.HBM)
    shape = jax.ShapeDtypeStruct
    arrays = [x, coef, labels.reshape(1, rows), pid.reshape(1, rows), slot_of.reshape(1, clusters)]
    return pl.pallas_call(
        functools.partial(first_kernel, per_owner, blk, chunks),
        in_specs=[pl.BlockSpec(memory_space=pltpu.SMEM)] + [hbm] * 5,
        out_specs=[VMEM_SPEC] * 6,
        out_shape=[
            shape((rows, feat), BF16),
            shape((1, rows), F32),
            shape((clusters // 2, feat), F32),
            shape((clusters // 2, feat), F32),
            shape((feat // 4, feat), BF16),
            shape((feat // 4, feat), F32),
        ],
        scratch_shapes=[
            pltpu.VMEM((feat // 2, rows), BF16),
            pltpu.VMEM((feat // 4, feat), F32),
            pltpu.VMEM((feat,), BF16),
            pltpu.VMEM((1, rows), jnp.int32),
            pltpu.VMEM((1, rows), jnp.int32),
            pltpu.VMEM((1, clusters), jnp.int32),
            pltpu.SemaphoreType.DMA((len(chunks),)),
            pltpu.SemaphoreType.DMA((4,)),
        ],
        compiler_params=pltpu.CompilerParams(vmem_limit_bytes=VMEM_LIMIT),
        name="scores_and_far",
    )(place, *[pltpu.with_memory_space_constraint(array, pltpu.HBM) for array in arrays])


def second(place, x, w, far_send, far_keep, blk, chunks=4):
    feat = x.shape[1]
    return pl.pallas_call(
        functools.partial(second_kernel, blk, chunks),
        in_specs=[pl.BlockSpec(memory_space=pltpu.SMEM)] + [VMEM_SPEC] * 4,
        out_specs=[VMEM_SPEC] * 2,
        out_shape=[
            jax.ShapeDtypeStruct((feat // 4, feat), BF16),
            jax.ShapeDtypeStruct((feat // 4, feat), F32),
        ],
        scratch_shapes=[pltpu.VMEM((feat // 2, feat), F32), pltpu.VMEM((feat // 2, feat // 2), F32)],
        compiler_params=pltpu.CompilerParams(vmem_limit_bytes=VMEM_LIMIT),
        name="near",
    )(place, x, w, far_send, far_keep)


def local(features, coef, labels, passage_id, slot_of):
    feat = features.shape[1]
    devices = lax.axis_size("rows")
    clusters = slot_of.shape[0]
    per_owner = clusters // devices
    blk = feat // devices
    me = lax.axis_index("rows").astype(jnp.int32)
    turn = LANES // blk
    core, parity = me & 1, (me & turn) // turn

    def swap(array, mask):
        return lax.ppermute(array, "rows", [(i, i ^ mask) for i in range(devices)])

    def rest(number):
        return (number // (2 * turn)) * (turn // 2) + (number % turn) // 2

    place = jnp.stack([core, parity])
    x, w, sums_send, sums_keep, far_send, far_keep = first(
        place, features, coef, labels, passage_id, slot_of, per_owner, blk
    )
    masks = [m for m in range(1, devices) if not m & 1 and not m & turn]
    masks = masks[1:2] + masks[:1] + masks[2:]
    far_in, sums_in = swap(far_send, 1), swap(sums_send, 1)
    far = (far_keep + far_in.astype(F32)).astype(BF16)
    sums = sums_keep + sums_in
    quarter = clusters // 4
    sums_far, sums_near = sums[:quarter].astype(BF16), sums[quarter:]
    w, _ = lax.optimization_barrier((w, (far, sums_far)))
    near_send, near_keep = second(place, x, w, far_send, far_keep, blk)
    near_in = swap(near_send, 1)
    sums = sums_near + swap(sums_far, turn).astype(F32)
    arrived = swap(far, turn)
    sums_out = sums.astype(BF16)
    sums_parts = [swap(sums_out, m) for m in sorted(masks)]
    near = near_keep + near_in.astype(F32) + arrived.astype(F32)
    block = lambda n: lax.dynamic_slice_in_dim(near, (rest(me) ^ n) * blk, blk, 0)
    hessian = block(0)
    parts = [block(rest(m)).astype(BF16) for m in masks]
    for part in sums_parts:
        sums = sums + part.astype(F32)
    sums, parts = lax.optimization_barrier((sums, parts))
    parts = [swap(part, m) for part, m in zip(parts, masks)]
    grad_local = lax.dynamic_slice_in_dim(sums, rest(me) * per_owner, per_owner, 0)
    sums = jnp.concatenate([sums, swap(sums, turn)], axis=0)
    stack = jnp.concatenate([sums, swap(sums, 1)], axis=0)
    columns = lax.dynamic_slice_in_dim(stack, me * blk, blk, 1)
    meat = lax.dot_general(
        columns,
        stack,
        (((0,), (0,)), ((), ())),
        precision=lax.Precision.HIGHEST,
        preferred_element_type=F32,
    )
    parts, meat = lax.optimization_barrier((parts, meat))
    for part in parts:
        hessian = hessian + part.astype(F32)
    return (hessian, meat, grad_local)


def solution(mesh):
    in_specs = (
        P(("groups", "rows"), None),
        P(),
        P(("groups", "rows")),
        P(("groups", "rows"), None),
        P("groups"),
    )
    out_specs = (
        P(("groups", "rows"), None),
        P(("groups", "rows"), None),
        P(("groups", "rows"), None),
    )
    return jax.shard_map(local, mesh=mesh, in_specs=in_specs, out_specs=out_specs, check_vma=False)
```

```python
import functools

import jax
import jax.numpy as jnp
from jax import lax
from jax.experimental import pallas as pl
from jax.experimental.pallas import tpu as pltpu
from jax.sharding import PartitionSpec as P

BF16 = jnp.bfloat16
F32 = jnp.float32
LANES = 128
VMEM_LIMIT = 20 * 1024 * 1024


def turned_block(x_ref, here, lane, weight):
    return (x_ref[here, pl.ds(lane, LANES)].T.astype(F32) * weight).astype(BF16)


def lane_of(block, parity):
    return pl.multiple_of((2 * block + parity) * LANES, LANES)


def core_rows(blk, core, pairs):
    for pair in range(pairs):
        base = 2 * pair * blk
        yield pl.ds(pair * blk, blk), [
            pl.ds(pl.multiple_of(base + number * blk, 16), blk) for number in (core, 1 - core)
        ]


def first_kernel(
    per_owner, blk, chunks, place, x_hbm, coef_hbm, label_hbm, pid_hbm, slot_hbm,
    x_ref, w_ref, sums_send, sums_keep, send_ref, keep_ref,
    left, send_acc, coef_ref, label_ref, pid_ref, slot_ref, x_sems, sems,
):
    core, parity = place[0], place[1]
    rows, feat = x_ref.shape
    clusters = slot_ref.shape[1]
    half = clusters // 2
    starts = [rows * sum(chunks[:n]) // sum(chunks) for n in range(len(chunks) + 1)]
    spans = [slice(a, b) for a, b in zip(starts, starts[1:])]
    small = [
        pltpu.make_async_copy(source, target, sems.at[n])
        for n, (source, target) in enumerate(
            [(coef_hbm, coef_ref), (slot_hbm, slot_ref), (label_hbm, label_ref), (pid_hbm, pid_ref)]
        )
    ]
    large = [
        pltpu.make_async_copy(x_hbm.at[here], x_ref.at[here], x_sems.at[n])
        for n, here in enumerate(spans)
    ]
    for copy in small:
        copy.start()
    for copy in large:
        copy.start()
    for copy in small:
        copy.wait()
    row = lax.broadcasted_iota(jnp.int32, (clusters, clusters), 0)
    turn = LANES // blk
    core_of = jnp.where(row >= half, core, 1 - core)
    inner = row % half
    parity_of = jnp.where(inner >= half // 2, parity, 1 - parity)
    inner = inner % (half // 2)
    rest = inner // per_owner
    owner = (rest // (turn // 2)) * (2 * turn) + parity_of * turn + (rest % (turn // 2)) * 2 + core_of
    slot = owner * per_owner + inner % per_owner
    passage = lax.broadcasted_iota(jnp.int32, (clusters, clusters), 1)
    names = jnp.sum(jnp.where(slot_ref[...] == slot, passage, 0), axis=1, keepdims=True)
    coef = jnp.broadcast_to(coef_ref[...].reshape(1, feat), (16, feat))
    def probabilities(n):
        here = spans[n]
        large[n].wait()
        logits = lax.dot_general(coef, x_ref[here, :], (((1,), (1,)), ((), ())), preferred_element_type=F32)[0:1]
        prob = 1.0 / (1.0 + jnp.exp(-logits))
        return prob * (1.0 - prob), label_ref[:, here].astype(F32) - prob

    def use(n, weight, score):
        here = spans[n]
        w_ref[:, here] = weight
        score = jnp.broadcast_to(score, (LANES, here.stop - here.start)).T
        score = jnp.concatenate([score] * (feat // LANES), axis=1)
        scored = (x_ref[here, :].astype(F32) * score).astype(BF16)
        member = jnp.where(pid_ref[:, here] == names, 1.0, 0.0).astype(BF16)
        sums = jnp.dot(member, scored, preferred_element_type=F32)
        for block in range(feat // (2 * LANES)):
            turned = turned_block(x_ref, here, lane_of(block, 1 - parity), weight)
            for pair in range(LANES // (2 * blk)):
                out = (block * LANES // (2 * blk) + pair) * blk
                for number in range(2):
                    start = out + jnp.where(core == number, 0, feat // 4)
                    at = (2 * pair + number) * blk
                    left[pl.ds(pl.multiple_of(start, 16), blk), here] = turned[at : at + blk]
        add(sums_send, sums[:half], n)
        add(sums_keep, sums[half:], n)

    def add(ref, term, n):
        if n:
            ref[...] += term
        else:
            ref[...] = term

    def multiply(n):
        term = jnp.dot(left[:, spans[n]], x_ref[spans[n], :], preferred_element_type=F32)
        add(keep_ref, term[: feat // 4], n)
        if n < len(spans) - 1:
            add(send_acc, term[feat // 4 :], n)
        else:
            term = term[feat // 4 :]
            send_ref[...] = (term + send_acc[...] if n else term).astype(BF16)

    held = probabilities(0)
    for n in range(len(spans)):
        ahead = probabilities(n + 1) if n + 1 < len(spans) else None
        use(n, *held)
        multiply(n)
        held = ahead


def second_kernel(blk, chunks, place, x_ref, w_ref, far_send, far_keep, send_ref, keep_ref, acc, cross):
    core, parity = place[0], place[1]
    rows, feat = x_ref.shape
    part = rows // chunks
    width = feat // (2 * LANES)
    for packed, (kept, sent) in core_rows(blk, core, feat // (4 * blk)):
        for b in range(width):
            lanes, lane = slice(b * LANES, (b + 1) * LANES), pl.ds(lane_of(b, parity), LANES)
            cross[kept, lanes] = far_keep[packed, lane]
            cross[sent, lanes] = far_send[packed, lane].astype(F32)
    total = corner = None
    middle = width * LANES // 2
    for n in range(chunks):
        here = slice(n * part, n * part + part)
        right = jnp.concatenate([x_ref[here, pl.ds(lane_of(b, parity), LANES)] for b in range(width)], axis=1)
        weight = w_ref[:, here]
        left = jnp.concatenate([turned_block(x_ref, here, lane_of(b, parity), weight) for b in range(width)], axis=0)
        term = jnp.dot(left[:middle], right, preferred_element_type=F32)
        total = term if total is None else total + term
        term = jnp.dot(left[middle:], right[:, middle:], preferred_element_type=F32)
        corner = term if corner is None else corner + term
    corner = jnp.concatenate([total[:, middle:].T, corner], axis=1)
    total = jnp.concatenate([total, corner], axis=0)
    turned = cross[...].T
    for b in range(width):
        lanes = slice(b * LANES, (b + 1) * LANES)
        acc[:, pl.ds(lane_of(b, parity), LANES)] = total[:, lanes]
        acc[:, pl.ds(lane_of(b, 1 - parity), LANES)] = turned[:, lanes]
    for packed, (kept, sent) in core_rows(blk, core, feat // (4 * blk)):
        keep_ref[packed, :] = acc[kept, :]
        send_ref[packed, :] = acc[sent, :].astype(BF16)


VMEM_SPEC = pl.BlockSpec(memory_space=pltpu.VMEM)


def first(place, x, coef, labels, pid, slot_of, per_owner, blk, chunks=(1, 2, 5)):
    rows, feat = x.shape
    clusters = slot_of.shape[0]
    hbm = pl.BlockSpec(memory_space=pltpu.HBM)
    shape = jax.ShapeDtypeStruct
    arrays = [x, coef, labels.reshape(1, rows), pid.reshape(1, rows), slot_of.reshape(1, clusters)]
    return pl.pallas_call(
        functools.partial(first_kernel, per_owner, blk, chunks),
        in_specs=[pl.BlockSpec(memory_space=pltpu.SMEM)] + [hbm] * 5,
        out_specs=[VMEM_SPEC] * 6,
        out_shape=[
            shape((rows, feat), BF16),
            shape((1, rows), F32),
            shape((clusters // 2, feat), F32),
            shape((clusters // 2, feat), F32),
            shape((feat // 4, feat), BF16),
            shape((feat // 4, feat), F32),
        ],
        scratch_shapes=[
            pltpu.VMEM((feat // 2, rows), BF16),
            pltpu.VMEM((feat // 4, feat), F32),
            pltpu.VMEM((feat,), BF16),
            pltpu.VMEM((1, rows), jnp.int32),
            pltpu.VMEM((1, rows), jnp.int32),
            pltpu.VMEM((1, clusters), jnp.int32),
            pltpu.SemaphoreType.DMA((len(chunks),)),
            pltpu.SemaphoreType.DMA((4,)),
        ],
        compiler_params=pltpu.CompilerParams(vmem_limit_bytes=VMEM_LIMIT),
        name="scores_and_far",
    )(place, *[pltpu.with_memory_space_constraint(array, pltpu.HBM) for array in arrays])


def second(place, x, w, far_send, far_keep, blk, chunks=4):
    feat = x.shape[1]
    return pl.pallas_call(
        functools.partial(second_kernel, blk, chunks),
        in_specs=[pl.BlockSpec(memory_space=pltpu.SMEM)] + [VMEM_SPEC] * 4,
        out_specs=[VMEM_SPEC] * 2,
        out_shape=[
            jax.ShapeDtypeStruct((feat // 4, feat), BF16),
            jax.ShapeDtypeStruct((feat // 4, feat), F32),
        ],
        scratch_shapes=[pltpu.VMEM((feat // 2, feat), F32), pltpu.VMEM((feat // 2, feat // 2), F32)],
        compiler_params=pltpu.CompilerParams(vmem_limit_bytes=VMEM_LIMIT),
        name="near",
    )(place, x, w, far_send, far_keep)


def local(features, coef, labels, passage_id, slot_of):
    feat = features.shape[1]
    devices = lax.axis_size("rows")
    clusters = slot_of.shape[0]
    per_owner = clusters // devices
    blk = feat // devices
    me = lax.axis_index("rows").astype(jnp.int32)
    turn = LANES // blk
    core, parity = me & 1, (me & turn) // turn

    def swap(array, mask):
        return lax.ppermute(array, "rows", [(i, i ^ mask) for i in range(devices)])

    def rest(number):
        return (number // (2 * turn)) * (turn // 2) + (number % turn) // 2

    place = jnp.stack([core, parity])
    x, w, sums_send, sums_keep, far_send, far_keep = first(
        place, features, coef, labels, passage_id, slot_of, per_owner, blk
    )
    masks = [m for m in range(1, devices) if not m & 1 and not m & turn]
    masks = masks[1:2] + masks[:1] + masks[2:]
    far_in, sums_in = swap(far_send, 1), swap(sums_send, 1)
    far = (far_keep + far_in.astype(F32)).astype(BF16)
    sums = sums_keep + sums_in
    quarter = clusters // 4
    sums_far, sums_near = sums[:quarter].astype(BF16), sums[quarter:]
    w, _ = lax.optimization_barrier((w, (far, sums_far)))
    near_send, near_keep = second(place, x, w, far_send, far_keep, blk)
    near_in = swap(near_send, 1)
    sums = sums_near + swap(sums_far, turn).astype(F32)
    arrived = swap(far, turn)
    sums_out = sums.astype(BF16)
    sums_parts = [swap(sums_out, m) for m in sorted(masks)]
    near = near_keep + near_in.astype(F32) + arrived.astype(F32)
    block = lambda n: lax.dynamic_slice_in_dim(near, (rest(me) ^ n) * blk, blk, 0)
    hessian = block(0)
    parts = [block(rest(m)).astype(BF16) for m in masks]
    for part in sums_parts:
        sums = sums + part.astype(F32)
    sums, _ = lax.optimization_barrier((sums, parts))
    parts = [swap(part, m) for part, m in zip(parts, masks)]
    grad_local = lax.dynamic_slice_in_dim(sums, rest(me) * per_owner, per_owner, 0)
    sums = jnp.concatenate([sums, swap(sums, turn)], axis=0)
    stack = jnp.concatenate([sums, swap(sums, 1)], axis=0)
    columns = lax.dynamic_slice_in_dim(stack, me * blk, blk, 1)
    meat = lax.dot_general(
        columns,
        stack,
        (((0,), (0,)), ((), ())),
        precision=lax.Precision.HIGHEST,
        preferred_element_type=F32,
    )
    parts, meat = lax.optimization_barrier((parts, meat))
    for part in parts:
        hessian = hessian + part.astype(F32)
    return (hessian, meat, grad_local)


def solution(mesh):
    in_specs = (
        P(("groups", "rows"), None),
        P(),
        P(("groups", "rows")),
        P(("groups", "rows"), None),
        P("groups"),
    )
    out_specs = (
        P(("groups", "rows"), None),
        P(("groups", "rows"), None),
        P(("groups", "rows"), None),
    )
    return jax.shard_map(local, mesh=mesh, in_specs=in_specs, out_specs=out_specs, check_vma=False)
```
